512 devices in a mesh: row: 32 (over x, z_lo, core), col: 16 (over z_hi, y).
Axes of the slice: x: 4, y: 4, z: 16 (z_hi: 4, z_lo: 4; z = z_hi * 4 + z_lo), core: 2. Of those that a mesh axis runs over, the one named last changes fastest.
Arguments:
- transmission: float32 [2, 2, 2048, 4096], P(None, None, 'row', 'col'), may hold values from -0.5 to 1.5
- probe: float32 [2, 128, 128], replicated, may hold values from -6 to 6
- prop_phase: float32 [128, 128], replicated, may hold values from -3.140625 to 3.140625
- intensity: bfloat16 [2048, 128, 128], P(('row', 'col')), may hold values from 0.049804688 to 4
- offsets: int32 [2048, 2], P(('row', 'col')), may hold values from 0 to 256, as said below
- counts: int32 [512], P(('row', 'col')), may hold values from 1 to 4, as said below
Outputs:
- object_grad: float32 [2, 2, 2048, 4096], P(None, None, 'row', 'col')
- probe_grad: float32 [2, 128, 128], replicated
The draws below stay inside these ranges and needn't reach their ends.
Inputs may be any that keep to these rules, and one draw needn't show every extreme that they name: offsets[q, 0] lies within 0 to 64 and offsets[q, 1] within 0 to 256, so a window lies in its own tile and the 64 cells around it; both ends are reached. `counts`: some device has all 4 slots live.
All inputs are finite; a program needn't handle non-finite values.
Results may differ from the reference program's by a relative error of at most 0.0003.
Values sent between devices are 32-bit elements; how exact they have to be, the bound alone decides.
A program may use at most 64 MiB of HBM per device.

```python
import math
import jax
import jax.numpy as jnp
from jax import lax

PIX = 128
HALO = 64
SLICES = 2
TILE_ROWS = 64
TILE_COLS = 256
SLOTS_DEV = 4
SLOTS = 2048
OBJ_ROWS = 2048
OBJ_COLS = 4096
N_ROW = 32
N_COL = 16


def draw_transmission(key, part):
    key = jax.random.fold_in(key, 5)
    first, second = jax.random.split(key)
    shape = (SLICES, OBJ_ROWS, OBJ_COLS)
    real_part = jnp.clip(0.9 + 0.15 * jax.random.normal(first, shape, jnp.float32), 0.4, 1.4)
    imag_part = jnp.clip(0.2 * jax.random.normal(second, shape, jnp.float32), -0.45, 0.45)
    return jnp.stack([real_part, imag_part]).astype(jnp.float32)


def draw_offsets(key, part):
    key = jax.random.fold_in(key, 11)
    first, second, third = jax.random.split(key, 3)
    row_part = jax.random.randint(first, (SLOTS,), 0, TILE_ROWS + 1)
    col_part = jax.random.randint(second, (SLOTS,), 0, TILE_COLS + 1)
    picks = jax.random.randint(third, (4,), 0, SLOTS)
    row_part = row_part.at[picks[0]].set(TILE_ROWS).at[picks[1]].set(0)
    col_part = col_part.at[picks[2]].set(TILE_COLS).at[picks[3]].set(0)
    return jnp.stack([row_part, col_part], axis=1).astype(jnp.int32)


def draw_counts(key, part):
    key = jax.random.fold_in(key, 17)
    first, second, third = jax.random.split(key, 3)
    devices = SLOTS // SLOTS_DEV
    upper = jax.random.randint(first, (devices,), 0, SLOTS_DEV)
    lower = jax.random.randint(second, (devices,), 0, SLOTS_DEV)
    counts = jnp.minimum(upper, lower) + 1
    chosen = jax.random.randint(third, (), 0, devices)
    return counts.at[chosen].set(SLOTS_DEV).astype(jnp.int32)


def shard_levels(stream_key, dims, cuts, least, largest):
    factor_of, own = 1.0, jax.random.fold_in(stream_key, 6)
    for axis_at, shards_of in cuts:
        draws = jnp.exp(jax.random.uniform(jax.random.fold_in(own, axis_at), (shards_of,), jnp.float32, least / len(cuts), largest / len(cuts)))
        factor_of = factor_of * jnp.repeat(draws, dims[axis_at] // shards_of).reshape([-1 if axis == axis_at else 1 for axis in range(len(dims))])
    return factor_of


def gaussian(rng, shape, scale, bound, held_as=jnp.bfloat16):
    return jnp.clip(scale * jax.random.normal(rng, shape, jnp.float32), -bound, bound).astype(held_as)


def setup_inputs(seed: int = 0) -> dict:
    key_list = jax.random.split(jax.random.key(seed), 7)
    transmission = draw_transmission(jax.random.fold_in(key_list[6], 71), 0)
    probe = gaussian(key_list[1], (2, PIX, PIX), 1.0, 6.0, jnp.float32)
    prop_phase = jnp.clip(jax.random.uniform(key_list[2], (PIX, PIX), jnp.float32, -3.140625, 3.140625), -3.140625, 3.140625)
    intensity = jnp.clip(jnp.exp(math.log(4.0) - 4.3859405 * jax.random.uniform(key_list[3], (SLOTS, PIX, PIX), jnp.float32) ** shard_levels(key_list[3], (SLOTS, PIX, PIX), ((0, 512),), -0.2, 0.2)), 0.049804688, 4.0).astype(jnp.bfloat16)
    offsets = draw_offsets(jax.random.fold_in(key_list[6], 71), 0)
    counts = draw_counts(jax.random.fold_in(key_list[6], 71), 0)
    return dict(transmission=transmission, probe=probe, prop_phase=prop_phase, intensity=intensity, offsets=offsets, counts=counts)


def dft_tables(side):
    index = jnp.arange(side, dtype=jnp.int32)
    product = index[:, None] * index[None, :] % side
    angles = product.astype(jnp.float32) * (-2.0 * math.pi / side)
    factor = 1.0 / math.sqrt(side)
    return (jnp.cos(angles) * factor, jnp.sin(angles) * factor)

def complex_mul(left_re, left_im, right_re, right_im):
    return (left_re * right_re - left_im * right_im, left_re * right_im + left_im * right_re)

def transform(field_re, field_im, table_re, table_im):
    high = lax.Precision.HIGHEST
    step_re = jnp.einsum('jk,kl->jl', field_re, table_re, precision=high) - jnp.einsum('jk,kl->jl', field_im, table_im, precision=high)
    step_im = jnp.einsum('jk,kl->jl', field_re, table_im, precision=high) + jnp.einsum('jk,kl->jl', field_im, table_re, precision=high)
    out_re = jnp.einsum('jk,kl->jl', table_re, step_re, precision=high) - jnp.einsum('jk,kl->jl', table_im, step_im, precision=high)
    out_im = jnp.einsum('jk,kl->jl', table_re, step_im, precision=high) + jnp.einsum('jk,kl->jl', table_im, step_re, precision=high)
    return (out_re, out_im)

def slot_loss(probe, patch, measured, propagator, table_re, table_im):
    wave_re, wave_im = (probe[0], probe[1])
    layers = patch.shape[1]
    for layer in range(layers):
        mixed_re, mixed_im = complex_mul(wave_re, wave_im, patch[0, layer], patch[1, layer])
        freq_re, freq_im = transform(mixed_re, mixed_im, table_re, table_im)
        if layer + 1 < layers:
            moved_re, moved_im = complex_mul(freq_re, freq_im, propagator[0], propagator[1])
            wave_re, wave_im = transform(moved_re, moved_im, table_re, -table_im)
    power = freq_re * freq_re + freq_im * freq_im
    return 0.5 * jnp.sum((power - measured) ** 2)

def batch_loss(probe, patches, measured, propagator, weights, table_re, table_im):
    losses = jax.vmap(slot_loss, in_axes=(None, 0, 0, None, None, None))(probe, patches, measured, propagator, table_re, table_im)
    return jnp.sum(weights * losses)

def reference(transmission, probe, prop_phase, intensity, offsets, counts):
    table_re, table_im = dft_tables(PIX)
    propagator = jnp.stack([jnp.cos(prop_phase), jnp.sin(prop_phase)])
    padded = jnp.pad(transmission, ((0, 0), (0, 0), (HALO, HALO), (HALO, HALO)))
    devices = N_ROW * N_COL
    zero = jnp.zeros((), jnp.int32)
    shape = (2, SLICES, PIX, PIX)

    def block(carry, item):
        grad_pad, probe_sum = carry
        offs, measured, count, device = item
        base_row = device // N_COL * TILE_ROWS
        base_col = device % N_COL * TILE_COLS
        weights = (jnp.arange(SLOTS_DEV, dtype=jnp.int32) < count).astype(jnp.float32)

        def take(offset):
            return lax.dynamic_slice(padded, (zero, zero, base_row + offset[0], base_col + offset[1]), shape)
        patches = jax.vmap(take)(offs)
        grad_probe, grad_patch = jax.grad(batch_loss, argnums=(0, 1))(probe, patches, measured.astype(jnp.float32), propagator, weights, table_re, table_im)

        def add_one(slot, grid):
            start = (zero, zero, base_row + offs[slot, 0], base_col + offs[slot, 1])
            current = lax.dynamic_slice(grid, start, shape)
            return lax.dynamic_update_slice(grid, current + grad_patch[slot], start)
        grad_pad = lax.fori_loop(0, SLOTS_DEV, add_one, grad_pad)
        return ((grad_pad, probe_sum + grad_probe), None)
    items = (offsets.reshape(devices, SLOTS_DEV, 2), intensity.reshape(devices, SLOTS_DEV, PIX, PIX), counts, jnp.arange(devices, dtype=jnp.int32))
    start = (jnp.zeros(padded.shape, jnp.float32), jnp.zeros(probe.shape, jnp.float32))
    (grad_pad, probe_sum), _ = lax.scan(block, start, items)
    object_grad = grad_pad[:, :, HALO:HALO + OBJ_ROWS, HALO:HALO + OBJ_COLS]
    return (object_grad, probe_sum / math.sqrt(SLOTS))
```

```python
import functools
import math

import jax
import jax.numpy as jnp
import ml_dtypes
import numpy as np
from jax import lax
from jax.experimental import pallas as pl
from jax.experimental.pallas import tpu as pltpu
from jax.sharding import PartitionSpec as P

MESH = pl.DeviceIdType.MESH
SIDE = 128
HALF = 64
TILES = 3


def dft_tables():
    index = np.arange(SIDE)
    angles = (index[:, None] * index[None, :] % SIDE) * (-2.0 * math.pi / SIDE)
    re, im = np.cos(angles) / math.sqrt(SIDE), np.sin(angles) / math.sqrt(SIDE)
    wide = np.block([[re, im], [-im, re]])
    parts = []
    for table in (wide, wide.T):
        high = table.astype(ml_dtypes.bfloat16)
        parts += [high, (table - high.astype(np.float64)).astype(ml_dtypes.bfloat16)]
    return np.stack(parts)


def halves(value):
    high = value.astype(jnp.bfloat16)
    return high, (value - high.astype(jnp.float32)).astype(jnp.bfloat16)


def product(left, right):
    dot = functools.partial(jnp.dot, preferred_element_type=jnp.float32)
    return dot(left[0], right[0]) + dot(left[1], right[0]) + dot(left[0], right[1])


def along_lanes(re, im, table):
    out = product(halves(jnp.concatenate([re, im], axis=1)), table)
    return out[:, :SIDE], out[:, SIDE:]


def along_rows(re, im, table):
    slots = re.shape[0] // SIDE
    beside = lambda part: jnp.concatenate([part[s * SIDE : (s + 1) * SIDE] for s in range(slots)], axis=1)
    out = product(table, halves(jnp.concatenate([beside(re), beside(im)], axis=0)))
    below = lambda part: jnp.concatenate([part[:, s * SIDE : (s + 1) * SIDE] for s in range(slots)], axis=0)
    return below(out[:SIDE]), below(out[SIDE:])


def times(a_re, a_im, b_re, b_im):
    return a_re * b_re - a_im * b_im, a_re * b_im + a_im * b_re


def times_conj(a_re, a_im, b_re, b_im):
    return a_re * b_re + a_im * b_im, a_im * b_re - a_re * b_im


def remote(src, dst, send, recv, device):
    return pltpu.make_async_remote_copy(
        src_ref=src, dst_ref=dst, send_sem=send, recv_sem=recv, device_id=device, device_id_type=MESH
    )


def kernel(
    rows, cols, total_slots,
    offsets, counts, trans, probe_in, phase_in, intensity_in, tables_in,
    object_out, probe_out,
    ext_first, ext_second, probe, phase, intensity, tables, edge_out, edge_in, patch, wave, prop, place, grid, fold_in, rim_out, rim_in,
    sum_out, sum_in, col_in, gathered,
    load_sem, edge_send, edge_recv, row_send, row_recv, fold_send, fold_recv, rim_send, rim_recv, sum_send, sum_recv,
):
    ext = (ext_first, ext_second)
    slots = intensity.shape[0]
    row, col = lax.axis_index("row"), lax.axis_index("col")
    up, down = lax.rem(row + rows - 1, rows), lax.rem(row + 1, rows)
    left, right = lax.rem(col + cols - 1, cols), lax.rem(col + 1, cols)
    lane = lax.broadcasted_iota(jnp.int32, (HALF, SIDE), 1)
    low = lane < HALF
    own = slice(HALF, 2 * HALF)

    own_loads = [
        [
            pltpu.make_async_copy(
                trans.at[:, layer, :, pl.ds(tile * SIDE, SIDE)], ext[layer].at[:, tile, own, :], load_sem.at[layer * 2 + tile]
            )
            for tile in range(2)
        ]
        for layer in range(2)
    ]
    small_loads = [
        pltpu.make_async_copy(src, dst, load_sem.at[4 + i])
        for i, (src, dst) in enumerate(
            [(phase_in, phase), (probe_in, probe), (tables_in, tables), (intensity_in, intensity)]
        )
    ]
    for layer in own_loads:
        for copy in layer:
            copy.start()
    for copy in small_loads:
        copy.start()

    barrier = pltpu.get_barrier_semaphore()

    def greet_row(k, _):
        pl.semaphore_signal(barrier, inc=1, device_id={"row": lax.rem(row + k, rows)}, device_id_type=MESH)
        return 0

    def greet_col(k, _):
        pl.semaphore_signal(barrier, inc=1, device_id={"col": lax.rem(col + k, cols)}, device_id_type=MESH)
        return 0

    lax.fori_loop(1, rows, greet_row, 0)
    lax.fori_loop(1, cols, greet_col, 0)
    pl.semaphore_wait(barrier, rows + cols - 2)

    def edge_copies(layer):
        return [
            remote(edge_out.at[layer, 0], edge_in.at[layer, 0], edge_send.at[layer, 0], edge_recv.at[layer, 0], {"col": right}),
            remote(edge_out.at[layer, 1], edge_in.at[layer, 1], edge_send.at[layer, 1], edge_recv.at[layer, 1], {"col": left}),
        ]

    def row_copies(layer, part):
        tiles = slice(0, 2) if part == 0 else slice(2, 3)
        src = ext[layer].at[:, tiles, own, :]
        return [
            remote(
                src, ext[layer].at[:, tiles, 0:HALF, :],
                row_send.at[layer, part, 0], row_recv.at[layer, part, 0], {"row": down},
            ),
            remote(
                src, ext[layer].at[:, tiles, 2 * HALF : 3 * HALF, :],
                row_send.at[layer, part, 1], row_recv.at[layer, part, 1], {"row": up},
            ),
        ]

    def start(copies):
        for copy in copies:
            copy.start()

    def landed(copies):
        for copy in copies:
            copy.wait_recv()

    def sent(copies):
        for copy in copies:
            copy.wait_send()

    for layer in range(2):
        for copy in own_loads[layer]:
            copy.wait()
        edge_out[layer, 0] = jnp.where(
            low, pltpu.roll(ext[layer][1, 1, own, :], HALF, 1), ext[layer][0, 1, own, :]
        )
        edge_out[layer, 1] = jnp.where(
            low, ext[layer][0, 0, own, :], pltpu.roll(ext[layer][1, 0, own, :], HALF, 1)
        )
        start(edge_copies(layer))
        start(row_copies(layer, 0))

    for layer in range(2):
        landed(edge_copies(layer))
        from_left = jnp.where(col > 0, edge_in[layer, 0], 0.0)
        from_right = jnp.where(col < cols - 1, edge_in[layer, 1], 0.0)
        ext[layer][0, 2, own, :] = jnp.where(low, from_right, from_left)
        ext[layer][1, 2, own, :] = pltpu.roll(jnp.where(low, from_left, from_right), HALF, 1)
        start(row_copies(layer, 1))

    place[:, :, :, 0:2, 0:HALF, :] = jnp.zeros(place.shape[:3] + (2, HALF, SIDE), jnp.float32)
    place[:, :, :, 0:2, 3 * HALF :, :] = jnp.zeros(place.shape[:3] + (2, HALF, SIDE), jnp.float32)
    place[:, :, :, 2, :, :] = jnp.zeros(place.shape[:3] + (4 * HALF, SIDE), jnp.float32)
    for copy in small_loads:
        copy.wait()
    prop[0] = jnp.cos(phase[...])
    prop[1] = jnp.sin(phase[...])

    lanes = lax.broadcasted_iota(jnp.int32, (SIDE, SIDE), 1)

    def spot(slot):
        across = offsets[slot, 1] + (TILES * SIDE - HALF)
        tile = lax.rem(lax.div(across, SIDE), TILES)
        return offsets[slot, 0], tile, lax.rem(tile + 1, TILES), lax.rem(across, SIDE)

    spots = [spot(slot) for slot in range(slots)]

    def rows_arrived(layer):
        landed(row_copies(layer, 0))
        landed(row_copies(layer, 1))

        @pl.when(row == 0)
        def _():
            ext[layer][:, :, 0:HALF, :] = jnp.zeros((2, TILES, HALF, SIDE), jnp.float32)

        @pl.when(row == rows - 1)
        def _():
            ext[layer][:, :, 2 * HALF :, :] = jnp.zeros((2, TILES, HALF, SIDE), jnp.float32)

    def gather(layer):
        for slot, (top, tile, after, shift) in enumerate(spots):
            back = lax.rem(SIDE - shift, SIDE)
            for part in range(2):
                first = ext[layer][part, tile, pl.ds(top, SIDE), :]
                second = ext[layer][part, after, pl.ds(top, SIDE), :]
                patch[layer, part, slot * SIDE : (slot + 1) * SIDE, :] = pltpu.roll(
                    jnp.where(lanes < shift, second, first), back, 1
                )

    def scatter(layer, grad):
        for slot, (_, _, _, shift) in enumerate(spots):
            for part in range(2):
                moved = pltpu.roll(grad[part][slot * SIDE : (slot + 1) * SIDE], shift, 1)
                place[layer, part, slot, 0, HALF : 3 * HALF, :] = jnp.where(lanes < shift, 0.0, moved)
                place[layer, part, slot, 1, HALF : 3 * HALF, :] = jnp.where(lanes < shift, moved, 0.0)
        for tile in reversed(range(TILES)):
            for part in range(2):
                total = None
                for slot, (top, first, second, _) in enumerate(spots):
                    which = jnp.where(first == tile, 0, jnp.where(second == tile, 1, 2))
                    term = place[layer, part, slot, which, pl.ds(HALF - top, 3 * HALF), :]
                    total = term if total is None else total + term
                grid[layer, part, tile] = total
            if tile == 2:
                start(fold_copies(layer, 1))
        start(fold_copies(layer, 0))

    def fold_copies(layer, part):
        tiles = slice(0, 2) if part == 0 else slice(2, 3)
        return [
            remote(
                grid.at[layer, :, tiles, 2 * HALF : 3 * HALF, :], fold_in.at[layer, 0, :, tiles],
                fold_send.at[layer, part, 0], fold_recv.at[layer, part, 0], {"row": down},
            ),
            remote(
                grid.at[layer, :, tiles, 0:HALF, :], fold_in.at[layer, 1, :, tiles],
                fold_send.at[layer, part, 1], fold_recv.at[layer, part, 1], {"row": up},
            ),
        ]

    def rim_copies(layer):
        return [
            remote(rim_out.at[layer, 0], rim_in.at[layer, 0], rim_send.at[layer, 0], rim_recv.at[layer, 0], {"col": right}),
            remote(rim_out.at[layer, 1], rim_in.at[layer, 1], rim_send.at[layer, 1], rim_recv.at[layer, 1], {"col": left}),
        ]

    repeat = lambda part: jnp.concatenate([part] * slots, axis=0)
    wide = (tables[0], tables[1])
    tall = (tables[2], tables[3])

    def transform(field):
        return along_rows(*along_lanes(*field, wide), tall)

    def inverse(field):
        return along_rows(*along_lanes(*field, tall), wide)

    shone = (repeat(probe[0]), repeat(probe[1]))
    moved = (repeat(prop[0]), repeat(prop[1]))

    rows_arrived(0)
    gather(0)
    field = times(*shone, patch[0, 0], patch[0, 1])
    field = inverse(times(*transform(field), *moved))
    wave[0] = field[0]
    wave[1] = field[1]
    rows_arrived(1)
    gather(1)
    far = transform(times(*field, patch[1, 0], patch[1, 1]))
    live = jnp.concatenate(
        [jnp.full((SIDE, SIDE), jnp.where(slot < counts[0], 2.0, 0.0), jnp.float32) for slot in range(slots)], axis=0
    )
    measured = jnp.concatenate([intensity[slot].astype(jnp.float32) for slot in range(slots)], axis=0)
    excess = (far[0] * far[0] + far[1] * far[1] - measured) * live
    back = inverse((far[0] * excess, far[1] * excess))
    scatter(1, times_conj(*back, wave[0], wave[1]))
    back = transform(times_conj(*back, patch[1, 0], patch[1, 1]))
    back = inverse(times_conj(*back, *moved))
    probe_grad = times_conj(*back, patch[0, 0], patch[0, 1])

    scale = 1.0 / math.sqrt(total_slots)
    for part in range(2):
        acc = probe_grad[part][:SIDE]
        for slot in range(1, slots):
            acc = acc + probe_grad[part][slot * SIDE : (slot + 1) * SIDE]
        sum_out[part * SIDE : (part + 1) * SIDE, :] = acc * scale
    depth = 2 * SIDE // rows
    piece = lambda k: pl.ds(pl.multiple_of(k * depth, depth), depth)

    def scatter_piece(k):
        other = lax.rem(row + k, rows)
        return remote(sum_out.at[piece(other)], sum_in.at[row], sum_send.at[0], sum_recv.at[0], {"row": other})

    def share_piece(k):
        return remote(col_in.at[col], col_in.at[col], sum_send.at[1], sum_recv.at[1], {"col": lax.rem(col + k, cols)})

    def spread_piece(k):
        return remote(
            gathered.at[piece(row)], gathered.at[piece(row)], sum_send.at[2], sum_recv.at[2], {"row": lax.rem(row + k, rows)}
        )

    def start_all(copy, count):
        def go(k, _):
            copy(k).start()
            return 0

        lax.fori_loop(1, count, go, 0)

    def wait_bytes(ref, sem):
        pltpu.make_async_copy(ref, ref, sem).wait()

    start_all(scatter_piece, rows)
    scatter(0, times_conj(*back, *shone))

    wait_bytes(sum_in.at[pl.ds(0, rows - 1)], sum_recv.at[0])
    sum_in[row] = sum_out[piece(row), :]
    col_in[col] = jnp.sum(sum_in[...], axis=0)
    start_all(share_piece, cols)

    def fold(layer, tile, part):
        above = jnp.where(row > 0, fold_in[layer, 0, part, tile], 0.0)
        below = jnp.where(row < rows - 1, fold_in[layer, 1, part, tile], 0.0)
        return grid[layer, part, tile, own, :] + above + below

    for layer in (1, 0):
        landed(fold_copies(layer, 1))
        re, im = fold(layer, 2, 0), fold(layer, 2, 1)
        turned = pltpu.roll(im, HALF, 1)
        rim_out[layer, 0] = jnp.where(low, re, turned)
        rim_out[layer, 1] = jnp.where(low, turned, re)
        start(rim_copies(layer))

    wait_bytes(col_in.at[pl.ds(0, cols - 1)], sum_recv.at[1])
    wait_bytes(col_in.at[pl.ds(0, cols - 1)], sum_send.at[1])
    gathered[piece(row), :] = jnp.sum(col_in[...], axis=0)
    start_all(spread_piece, rows)

    for layer in (1, 0):
        landed(fold_copies(layer, 0))
        landed(rim_copies(layer))
        from_left = jnp.where(col > 0, rim_in[layer, 0], 0.0)
        from_right = jnp.where(col < cols - 1, rim_in[layer, 1], 0.0)
        for part in range(2):
            if part == 1:
                from_left, from_right = pltpu.roll(from_left, HALF, 1), pltpu.roll(from_right, HALF, 1)
            object_out[part, layer, :, 0:SIDE] = fold(layer, 0, part) + jnp.where(low, from_left, 0.0)
            object_out[part, layer, :, SIDE:] = fold(layer, 1, part) + jnp.where(low, 0.0, from_right)

    rest = gathered.at[pl.ds(0, depth * (rows - 1))]
    wait_bytes(rest, sum_recv.at[2])
    for part in range(2):
        probe_out[part] = gathered[part * SIDE : (part + 1) * SIDE, :]

    wait_bytes(sum_in.at[pl.ds(0, rows - 1)], sum_send.at[0])
    wait_bytes(rest, sum_send.at[2])
    for layer in range(2):
        sent(edge_copies(layer))
        sent(rim_copies(layer))
        for part in range(2):
            sent(row_copies(layer, part))
            sent(fold_copies(layer, part))


def solution(mesh):
    rows, cols = mesh.shape["row"], mesh.shape["col"]

    def shards(transmission, probe, prop_phase, intensity, offsets, counts):
        slots = offsets.shape[0]
        tables = jnp.asarray(dft_tables())
        f32 = jnp.float32
        depth = 2 * SIDE // rows
        any_space = pl.BlockSpec(memory_space=pl.ANY)
        smem = pl.BlockSpec(memory_space=pltpu.SMEM)
        vmem = pl.BlockSpec(memory_space=pltpu.VMEM)
        dma = pltpu.SemaphoreType.DMA
        return pl.pallas_call(
            functools.partial(kernel, rows, cols, slots * rows * cols),
            out_shape=(
                jax.ShapeDtypeStruct(transmission.shape, f32),
                jax.ShapeDtypeStruct(probe.shape, f32),
            ),
            in_specs=[smem, smem] + [any_space] * 5,
            out_specs=(vmem, vmem),
            scratch_shapes=[
                pltpu.VMEM((2, TILES, 3 * HALF, SIDE), f32),
                pltpu.VMEM((2, TILES, 3 * HALF, SIDE), f32),
                pltpu.VMEM(probe.shape, f32),
                pltpu.VMEM(prop_phase.shape, f32),
                pltpu.VMEM(intensity.shape, intensity.dtype),
                pltpu.VMEM(tables.shape, tables.dtype),
                pltpu.VMEM((2, 2, HALF, SIDE), f32),
                pltpu.VMEM((2, 2, HALF, SIDE), f32),
                pltpu.VMEM((2, 2, slots * SIDE, SIDE), f32),
                pltpu.VMEM((2, slots * SIDE, SIDE), f32),
                pltpu.VMEM((2, SIDE, SIDE), f32),
                pltpu.VMEM((2, 2, slots, 3, 4 * HALF, SIDE), f32),
                pltpu.VMEM((2, 2, TILES, 3 * HALF, SIDE), f32),
                pltpu.VMEM((2, 2, 2, TILES, HALF, SIDE), f32),
                pltpu.VMEM((2, 2, HALF, SIDE), f32),
                pltpu.VMEM((2, 2, HALF, SIDE), f32),
                pltpu.VMEM((2 * SIDE, SIDE), f32),
                pltpu.VMEM((rows, depth, SIDE), f32),
                pltpu.VMEM((cols, depth, SIDE), f32),
                pltpu.VMEM((2 * SIDE, SIDE), f32),
                dma((8,)),
                dma((2, 2)),
                dma((2, 2)),
                dma((2, 2, 2)),
                dma((2, 2, 2)),
                dma((2, 2, 2)),
                dma((2, 2, 2)),
                dma((2, 2)),
                dma((2, 2)),
                dma((3,)),
                dma((3,)),
            ],
            compiler_params=pltpu.CompilerParams(
                collective_id=0, has_side_effects=True, vmem_limit_bytes=40 * 1024 * 1024
            ),
        )(offsets, counts, transmission, probe, prop_phase, intensity, tables)

    in_specs = (
        P(None, None, "row", "col"),
        P(),
        P(),
        P(("row", "col"), None, None),
        P(("row", "col"), None),
        P(("row", "col")),
    )
    out_specs = (P(None, None, "row", "col"), P())
    return jax.shard_map(shards, mesh=mesh, in_specs=in_specs, out_specs=out_specs, check_vma=False)
```

```python
import functools
import math

import jax
import jax.numpy as jnp
from jax import lax
from jax.experimental import pallas as pl
from jax.experimental.pallas import tpu as pltpu
from jax.sharding import PartitionSpec as P

MESH = pl.DeviceIdType.MESH
SIDE = 128
HALF = 64
TILES = 3
Z_LOW = 4
Y_SIDE = 4


def dft_tables():
    rows = lax.broadcasted_iota(jnp.int32, (SIDE, SIDE), 0)
    lanes = lax.broadcasted_iota(jnp.int32, (SIDE, SIDE), 1)
    angles = lax.rem(rows * lanes, SIDE).astype(jnp.float32) * (-2.0 * math.pi / SIDE)
    re, im = jnp.cos(angles) * (1.0 / math.sqrt(SIDE)), jnp.sin(angles) * (1.0 / math.sqrt(SIDE))
    block = lambda a, b, c, d: jnp.concatenate(
        [jnp.concatenate([a, b], axis=1), jnp.concatenate([c, d], axis=1)], axis=0
    )
    return block(re, im, -im, re), block(re, -im, im, re)


def halves(value):
    high = value.astype(jnp.bfloat16)
    return high, (value - high.astype(jnp.float32)).astype(jnp.bfloat16)


def product(left, right):
    dot = functools.partial(jnp.dot, preferred_element_type=jnp.float32)
    return dot(left[0], right[0]) + dot(left[1], right[0]) + dot(left[0], right[1])


def along_lanes(re, im, table):
    out = product(halves(jnp.concatenate([re, im], axis=1)), table)
    return out[:, :SIDE], out[:, SIDE:]


def along_rows(re, im, table):
    slots = re.shape[0] // SIDE
    beside = lambda part: jnp.concatenate([part[s * SIDE : (s + 1) * SIDE] for s in range(slots)], axis=1)
    out = product(table, halves(jnp.concatenate([beside(re), beside(im)], axis=0)))
    below = lambda part: jnp.concatenate([part[:, s * SIDE : (s + 1) * SIDE] for s in range(slots)], axis=0)
    return below(out[:SIDE]), below(out[SIDE:])


def times(a_re, a_im, b_re, b_im):
    return a_re * b_re - a_im * b_im, a_re * b_im + a_im * b_re


def times_conj(a_re, a_im, b_re, b_im):
    return a_re * b_re + a_im * b_im, a_im * b_re - a_re * b_im


def remote(src, dst, send, recv, device):
    return pltpu.make_async_remote_copy(
        src_ref=src, dst_ref=dst, send_sem=send, recv_sem=recv, device_id=device, device_id_type=MESH
    )


def kernel(
    rows, cols, total_slots,
    offsets, counts, trans, probe_in, phase_in, intensity_in,
    object_out, probe_out,
    ext_first, ext_second, probe, phase, intensity, tables, edge_out, edge_in, patch, wave, prop, place, grid, fold_in, rim_out, rim_in,
    sum_out, core_in, plane_out, plane_in, line_in, gathered,
    load_sem, edge_send, edge_recv, row_send, row_recv, fold_send, fold_recv, rim_send, rim_recv, sum_send, sum_recv, line_sem,
):
    ext = (ext_first, ext_second)
    slots = intensity.shape[0]
    row, col = lax.axis_index("row"), lax.axis_index("col")
    up, down = lax.rem(row + rows - 1, rows), lax.rem(row + 1, rows)
    left, right = lax.rem(col + cols - 1, cols), lax.rem(col + 1, cols)
    lane = lax.broadcasted_iota(jnp.int32, (HALF, SIDE), 1)
    low = lane < HALF
    own = slice(HALF, 2 * HALF)

    own_loads = [
        [
            pltpu.make_async_copy(
                trans.at[:, layer, :, pl.ds(tile * SIDE, SIDE)], ext[layer].at[:, tile, own, :], load_sem.at[layer * 2 + tile]
            )
            for tile in range(2)
        ]
        for layer in range(2)
    ]
    small_loads = [
        pltpu.make_async_copy(src, dst, load_sem.at[4 + i])
        for i, (src, dst) in enumerate(
            [(phase_in, phase), (probe_in, probe), (intensity_in, intensity)]
        )
    ]
    for layer in own_loads:
        for copy in layer:
            copy.start()
    for copy in small_loads:
        copy.start()

    x_side, line = rows // (2 * Z_LOW), Z_LOW * (cols // Y_SIDE)
    plane = x_side * Y_SIDE
    x, z_low, core = lax.div(row, 2 * Z_LOW), lax.rem(lax.div(row, 2), Z_LOW), lax.rem(row, 2)
    y, z = lax.rem(col, Y_SIDE), lax.div(col, Y_SIDE) * Z_LOW + z_low
    spot_in_plane = x * Y_SIDE + y

    def plane_peer(k):
        to_x = lax.rem(x + lax.div(k, Y_SIDE), x_side)
        to_y = lax.rem(y + lax.rem(k, Y_SIDE), Y_SIDE)
        return to_x * Y_SIDE + to_y, {"row": (to_x * Z_LOW + z_low) * 2 + core, "col": col - y + to_y}

    def line_peer(k):
        to_z = lax.rem(z + k, line)
        return {"row": (x * Z_LOW + lax.rem(to_z, Z_LOW)) * 2 + core, "col": lax.div(to_z, Z_LOW) * Y_SIDE + y}

    sibling = {"row": row + 1 - 2 * core, "col": col}

    barrier = pltpu.get_barrier_semaphore()

    def greet(device):
        pl.semaphore_signal(barrier, inc=1, device_id=device, device_id_type=MESH)

    def greet_plane(k, _):
        greet(plane_peer(k)[1])
        return 0

    for device in ({"row": up}, {"row": down}, {"col": left}, {"col": right}, line_peer(1), line_peer(line - 1)):
        greet(device)
    lax.fori_loop(1, plane, greet_plane, 0)

    reaches = []
    while 2 ** len(reaches) < line // 2:
        reaches.append(2 ** len(reaches))

    def line_signal(turn):
        if turn < len(reaches):
            for k in (reaches[turn], line - reaches[turn]):
                pl.semaphore_signal(line_sem.at[turn], inc=1, device_id=line_peer(k), device_id_type=MESH)

    def line_wait(turn):
        if turn < len(reaches):
            pl.semaphore_wait(line_sem.at[turn], 2)

    def edge_copies(layer):
        return [
            remote(edge_out.at[layer, 0], edge_in.at[layer, 0], edge_send.at[layer, 0], edge_recv.at[layer, 0], {"col": right}),
            remote(edge_out.at[layer, 1], edge_in.at[layer, 1], edge_send.at[layer, 1], edge_recv.at[layer, 1], {"col": left}),
        ]

    def row_copies(layer, part):
        tiles = slice(0, 2) if part == 0 else slice(2, 3)
        src = ext[layer].at[:, tiles, own, :]
        return [
            remote(
                src, ext[layer].at[:, tiles, 0:HALF, :],
                row_send.at[layer, part, 0], row_recv.at[layer, part, 0], {"row": down},
            ),
            remote(
                src, ext[layer].at[:, tiles, 2 * HALF : 3 * HALF, :],
                row_send.at[layer, part, 1], row_recv.at[layer, part, 1], {"row": up},
            ),
        ]

    def start(copies):
        for copy in copies:
            copy.start()

    def landed(copies):
        for copy in copies:
            copy.wait_recv()

    def sent(copies):
        for copy in copies:
            copy.wait_send()

    for layer in range(2):
        for copy in own_loads[layer]:
            copy.wait()
        edge_out[layer, 0] = jnp.where(
            low, pltpu.roll(ext[layer][1, 1, own, :], HALF, 1), ext[layer][0, 1, own, :]
        )
        edge_out[layer, 1] = jnp.where(
            low, ext[layer][0, 0, own, :], pltpu.roll(ext[layer][1, 0, own, :], HALF, 1)
        )
    pl.semaphore_wait(barrier, plane - 1 + 6)
    start(edge_copies(0))
    start(row_copies(0, 0))
    start(edge_copies(1))
    line_signal(0)

    for i, table in enumerate(dft_tables()):
        tables[2 * i], tables[2 * i + 1] = halves(table)
    for copy in small_loads:
        copy.wait()
    prop[0] = jnp.cos(phase[...])
    prop[1] = jnp.sin(phase[...])
    place[:, :, :, 0:2, 0:HALF, :] = jnp.zeros(place.shape[:3] + (2, HALF, SIDE), jnp.float32)
    place[:, :, :, 0:2, 3 * HALF :, :] = jnp.zeros(place.shape[:3] + (2, HALF, SIDE), jnp.float32)
    place[:, :, :, 2, :, :] = jnp.zeros(place.shape[:3] + (4 * HALF, SIDE), jnp.float32)
    line_wait(0)
    line_signal(1)

    for layer in range(2):
        landed(edge_copies(layer))
        from_left = jnp.where(col > 0, edge_in[layer, 0], 0.0)
        from_right = jnp.where(col < cols - 1, edge_in[layer, 1], 0.0)
        ext[layer][0, 2, own, :] = jnp.where(low, from_right, from_left)
        ext[layer][1, 2, own, :] = pltpu.roll(jnp.where(low, from_left, from_right), HALF, 1)
        start(row_copies(layer, 1))
        if layer == 0:
            start(row_copies(1, 0))
    line_wait(1)
    line_signal(2)

    lanes = lax.broadcasted_iota(jnp.int32, (SIDE, SIDE), 1)

    def spot(slot):
        across = offsets[1, slot] + (TILES * SIDE - HALF)
        tile = lax.rem(lax.div(across, SIDE), TILES)
        return offsets[0, slot], tile, lax.rem(tile + 1, TILES), lax.rem(across, SIDE)

    spots = [spot(slot) for slot in range(slots)]

    def rows_arrived(layer):
        landed(row_copies(layer, 0))
        landed(row_copies(layer, 1))

        @pl.when(row == 0)
        def _():
            ext[layer][:, :, 0:HALF, :] = jnp.zeros((2, TILES, HALF, SIDE), jnp.float32)

        @pl.when(row == rows - 1)
        def _():
            ext[layer][:, :, 2 * HALF :, :] = jnp.zeros((2, TILES, HALF, SIDE), jnp.float32)

    def gather(layer):
        for slot, (top, tile, after, shift) in enumerate(spots):
            back = lax.rem(SIDE - shift, SIDE)
            for part in range(2):
                first = ext[layer][part, tile, pl.ds(top, SIDE), :]
                second = ext[layer][part, after, pl.ds(top, SIDE), :]
                patch[layer, part, slot * SIDE : (slot + 1) * SIDE, :] = pltpu.roll(
                    jnp.where(lanes < shift, second, first), back, 1
                )

    def scatter(layer, grad):
        for slot, (_, _, _, shift) in enumerate(spots):
            for part in range(2):
                moved = pltpu.roll(grad[part][slot * SIDE : (slot + 1) * SIDE], shift, 1)
                place[layer, part, slot, 0, HALF : 3 * HALF, :] = jnp.where(lanes < shift, 0.0, moved)
                place[layer, part, slot, 1, HALF : 3 * HALF, :] = jnp.where(lanes < shift, moved, 0.0)
        for tile in reversed(range(TILES)):
            for part in range(2):
                total = None
                for slot, (top, first, second, _) in enumerate(spots):
                    which = jnp.where(first == tile, 0, jnp.where(second == tile, 1, 2))
                    term = place[layer, part, slot, which, pl.ds(HALF - top, 3 * HALF), :]
                    total = term if total is None else total + term
                grid[layer, part, tile] = total
            if tile == 2:
                start(fold_copies(layer, 1))
        start(fold_copies(layer, 0))

    def fold_copies(layer, part):
        tiles = slice(0, 2) if part == 0 else slice(2, 3)
        return [
            remote(
                grid.at[layer, :, tiles, 2 * HALF : 3 * HALF, :], fold_in.at[layer, 0, :, tiles],
                fold_send.at[layer, part, 0], fold_recv.at[layer, part, 0], {"row": down},
            ),
            remote(
                grid.at[layer, :, tiles, 0:HALF, :], fold_in.at[layer, 1, :, tiles],
                fold_send.at[layer, part, 1], fold_recv.at[layer, part, 1], {"row": up},
            ),
        ]

    def rim_copies(layer):
        return [
            remote(rim_out.at[layer, 0], rim_in.at[layer, 0], rim_send.at[layer, 0], rim_recv.at[layer, 0], {"col": right}),
            remote(rim_out.at[layer, 1], rim_in.at[layer, 1], rim_send.at[layer, 1], rim_recv.at[layer, 1], {"col": left}),
        ]

    repeat = lambda part: jnp.concatenate([part] * slots, axis=0)
    wide = (tables[0], tables[1])
    tall = (tables[2], tables[3])

    def transform(field):
        return along_rows(*along_lanes(*field, wide), tall)

    def inverse(field):
        return along_rows(*along_lanes(*field, tall), wide)

    shone = (repeat(probe[0]), repeat(probe[1]))
    moved = (repeat(prop[0]), repeat(prop[1]))

    rows_arrived(0)
    gather(0)
    field = times(*shone, patch[0, 0], patch[0, 1])
    field = inverse(times(*transform(field), *moved))
    wave[0] = field[0]
    wave[1] = field[1]
    rows_arrived(1)
    gather(1)
    far = transform(times(*field, patch[1, 0], patch[1, 1]))
    live = jnp.concatenate(
        [jnp.full((SIDE, SIDE), jnp.where(slot < counts[0], 2.0, 0.0), jnp.float32) for slot in range(slots)], axis=0
    )
    measured = jnp.concatenate([intensity[slot].astype(jnp.float32) for slot in range(slots)], axis=0)
    excess = (far[0] * far[0] + far[1] * far[1] - measured) * live
    back = inverse((far[0] * excess, far[1] * excess))
    scatter(1, times_conj(*back, wave[0], wave[1]))
    back = transform(times_conj(*back, patch[1, 0], patch[1, 1]))
    back = inverse(times_conj(*back, *moved))
    probe_grad = times_conj(*back, patch[0, 0], patch[0, 1])

    scale = 1.0 / math.sqrt(total_slots)
    for part in range(2):
        acc = probe_grad[part][:SIDE]
        for slot in range(1, slots):
            acc = acc + probe_grad[part][slot * SIDE : (slot + 1) * SIDE]
        sum_out[part] = acc * scale

    def wait_bytes(ref, sem):
        pltpu.make_async_copy(ref, ref, sem).wait()

    def start_all(copy, count):
        def go(k, _):
            copy(k).start()
            return 0

        lax.fori_loop(1, count, go, 0)

    halves_in = remote(sum_out.at[1 - core], core_in, sum_send.at[0], sum_recv.at[0], sibling)

    def scatter_piece(k):
        index, device = plane_peer(k)
        return remote(plane_out.at[index], plane_in.at[spot_in_plane], sum_send.at[1], sum_recv.at[1], device)

    def share_piece(k):
        return remote(line_in.at[z], line_in.at[z], sum_send.at[2], sum_recv.at[2], line_peer(k))

    def spread_piece(k):
        mine = gathered.at[core, spot_in_plane]
        return remote(mine, mine, sum_send.at[3], sum_recv.at[3], plane_peer(k)[1])

    halves_out = remote(gathered.at[core], gathered.at[core], sum_send.at[4], sum_recv.at[4], sibling)

    def fold(layer, tile, part):
        above = jnp.where(row > 0, fold_in[layer, 0, part, tile], 0.0)
        below = jnp.where(row < rows - 1, fold_in[layer, 1, part, tile], 0.0)
        return grid[layer, part, tile, own, :] + above + below

    def fold_rims(layer):
        landed(fold_copies(layer, 1))
        re, im = fold(layer, 2, 0), fold(layer, 2, 1)
        turned = pltpu.roll(im, HALF, 1)
        rim_out[layer, 0] = jnp.where(low, re, turned)
        rim_out[layer, 1] = jnp.where(low, turned, re)
        start(rim_copies(layer))

    def fold_tiles(layer):
        landed(fold_copies(layer, 0))
        landed(rim_copies(layer))
        from_left = jnp.where(col > 0, rim_in[layer, 0], 0.0)
        from_right = jnp.where(col < cols - 1, rim_in[layer, 1], 0.0)
        for part in range(2):
            if part == 1:
                from_left, from_right = pltpu.roll(from_left, HALF, 1), pltpu.roll(from_right, HALF, 1)
            object_out[part, layer, :, 0:SIDE] = fold(layer, 0, part) + jnp.where(low, from_left, 0.0)
            object_out[part, layer, :, SIDE:] = fold(layer, 1, part) + jnp.where(low, 0.0, from_right)

    halves_in.start()
    scatter(0, times_conj(*back, *shone))
    halves_in.wait_recv()
    plane_out[...] = (sum_out[core] + core_in[...]).reshape(plane_out.shape)
    start_all(scatter_piece, plane)
    plane_in[spot_in_plane] = plane_out[spot_in_plane]
    fold_rims(1)
    wait_bytes(plane_in.at[pl.ds(0, plane - 1)], sum_recv.at[1])
    line_in[z] = jnp.sum(plane_in[...], axis=0)
    line_wait(2)
    start_all(share_piece, line)
    fold_rims(0)
    fold_tiles(1)
    wait_bytes(line_in.at[pl.ds(0, line - 1)], sum_recv.at[2])
    gathered[core, spot_in_plane] = jnp.sum(line_in[...], axis=0)
    start_all(spread_piece, plane)
    fold_tiles(0)
    pieces = gathered.at[core, pl.ds(0, plane - 1)]
    wait_bytes(pieces, sum_recv.at[3])
    halves_out.start()
    halves_in.wait_send()
    wait_bytes(plane_in.at[pl.ds(0, plane - 1)], sum_send.at[1])
    wait_bytes(line_in.at[pl.ds(0, line - 1)], sum_send.at[2])
    wait_bytes(pieces, sum_send.at[3])
    for layer in range(2):
        sent(edge_copies(layer))
        sent(rim_copies(layer))
        for part in range(2):
            sent(row_copies(layer, part))
            sent(fold_copies(layer, part))
    halves_out.wait()
    probe_out[...] = gathered[...].reshape(probe_out.shape)


def solution(mesh):
    rows, cols = mesh.shape["row"], mesh.shape["col"]

    def shards(transmission, probe, prop_phase, intensity, offsets, counts):
        slots = offsets.shape[0]
        f32 = jnp.float32
        plane = rows // (2 * Z_LOW) * Y_SIDE
        line = Z_LOW * (cols // Y_SIDE)
        depth = SIDE // plane
        hbm = pl.BlockSpec(memory_space=pltpu.HBM)
        smem = pl.BlockSpec(memory_space=pltpu.SMEM)
        vmem = pl.BlockSpec(memory_space=pltpu.VMEM)
        dma = pltpu.SemaphoreType.DMA
        return pl.pallas_call(
            functools.partial(kernel, rows, cols, slots * rows * cols),
            out_shape=(
                jax.ShapeDtypeStruct(transmission.shape, f32),
                jax.ShapeDtypeStruct(probe.shape, f32),
            ),
            in_specs=[smem, smem] + [hbm] * 4,
            out_specs=(vmem, vmem),
            scratch_shapes=[
                pltpu.VMEM((2, TILES, 3 * HALF, SIDE), f32),
                pltpu.VMEM((2, TILES, 3 * HALF, SIDE), f32),
                pltpu.VMEM(probe.shape, f32),
                pltpu.VMEM(prop_phase.shape, f32),
                pltpu.VMEM(intensity.shape, intensity.dtype),
                pltpu.VMEM((4, 2 * SIDE, 2 * SIDE), jnp.bfloat16),
                pltpu.VMEM((2, 2, HALF, SIDE), f32),
                pltpu.VMEM((2, 2, HALF, SIDE), f32),
                pltpu.VMEM((2, 2, slots * SIDE, SIDE), f32),
                pltpu.VMEM((2, slots * SIDE, SIDE), f32),
                pltpu.VMEM((2, SIDE, SIDE), f32),
                pltpu.VMEM((2, 2, slots, 3, 4 * HALF, SIDE), f32),
                pltpu.VMEM((2, 2, TILES, 3 * HALF, SIDE), f32),
                pltpu.VMEM((2, 2, 2, TILES, HALF, SIDE), f32),
                pltpu.VMEM((2, 2, HALF, SIDE), f32),
                pltpu.VMEM((2, 2, HALF, SIDE), f32),
                pltpu.VMEM((2, SIDE, SIDE), f32),
                pltpu.VMEM((SIDE, SIDE), f32),
                pltpu.VMEM((plane, depth, SIDE), f32),
                pltpu.VMEM((plane, depth, SIDE), f32),
                pltpu.VMEM((line, depth, SIDE), f32),
                pltpu.VMEM((2, plane, depth, SIDE), f32),
                dma((7,)),
                dma((2, 2)),
                dma((2, 2)),
                dma((2, 2, 2)),
                dma((2, 2, 2)),
                dma((2, 2, 2)),
                dma((2, 2, 2)),
                dma((2, 2)),
                dma((2, 2)),
                dma((5,)),
                dma((5,)),
                pltpu.SemaphoreType.REGULAR((3,)),
            ],
            compiler_params=pltpu.CompilerParams(
                collective_id=0, has_side_effects=True, vmem_limit_bytes=60 * 1024 * 1024
            ),
        )(offsets.T, counts, transmission, probe, prop_phase, intensity)

    in_specs = (
        P(None, None, "row", "col"),
        P(),
        P(),
        P(("row", "col"), None, None),
        P(("row", "col"), None),
        P(("row", "col")),
    )
    out_specs = (P(None, None, "row", "col"), P())
    return jax.shard_map(shards, mesh=mesh, in_specs=in_specs, out_specs=out_specs, check_vma=False)
```

```python
import functools
import math

import jax
import jax.numpy as jnp
from jax import lax
from jax.experimental import pallas as pl
from jax.experimental.pallas import tpu as pltpu
from jax.sharding import PartitionSpec as P

MESH = pl.DeviceIdType.MESH
SIDE = 128
HALF = 64
TILES = 3
Z_LOW = 4
Y_SIDE = 4


def dft_tables():
    rows = lax.broadcasted_iota(jnp.int32, (SIDE, SIDE), 0)
    lanes = lax.broadcasted_iota(jnp.int32, (SIDE, SIDE), 1)
    angles = lax.rem(rows * lanes, SIDE).astype(jnp.float32) * (-2.0 * math.pi / SIDE)
    re, im = jnp.cos(angles) * (1.0 / math.sqrt(SIDE)), jnp.sin(angles) * (1.0 / math.sqrt(SIDE))
    block = lambda a, b, c, d: jnp.concatenate(
        [jnp.concatenate([a, b], axis=1), jnp.concatenate([c, d], axis=1)], axis=0
    )
    return block(re, im, -im, re), block(re, -im, im, re)


def halves(value):
    high = value.astype(jnp.bfloat16)
    return high, (value - high.astype(jnp.float32)).astype(jnp.bfloat16)


def product(left, right):
    dot = functools.partial(jnp.dot, preferred_element_type=jnp.float32)
    return dot(left[0], right[0]) + dot(left[1], right[0]) + dot(left[0], right[1])


def along_lanes(re, im, table):
    out = product(halves(jnp.concatenate([re, im], axis=1)), table)
    return out[:, :SIDE], out[:, SIDE:]


def along_rows(re, im, table):
    slots = re.shape[0] // SIDE
    beside = lambda part: jnp.concatenate([part[s * SIDE : (s + 1) * SIDE] for s in range(slots)], axis=1)
    out = product(table, halves(jnp.concatenate([beside(re), beside(im)], axis=0)))
    below = lambda part: jnp.concatenate([part[:, s * SIDE : (s + 1) * SIDE] for s in range(slots)], axis=0)
    return below(out[:SIDE]), below(out[SIDE:])


def times(a_re, a_im, b_re, b_im):
    return a_re * b_re - a_im * b_im, a_re * b_im + a_im * b_re


def times_conj(a_re, a_im, b_re, b_im):
    return a_re * b_re + a_im * b_im, a_im * b_re - a_re * b_im


def remote(src, dst, send, recv, device):
    return pltpu.make_async_remote_copy(
        src_ref=src, dst_ref=dst, send_sem=send, recv_sem=recv, device_id=device, device_id_type=MESH
    )


def kernel(
    rows, cols, total_slots,
    offsets, counts, trans, probe_in, phase_in, intensity_in,
    object_out, probe_out,
    ext_first, ext_second, probe, phase, intensity, tables, edge_out, edge_in, patch, wave, prop, place, grid, fold_in, rim_out, rim_in,
    sum_out, core_in, plane_out, plane_in, line_in, gathered,
    load_sem, edge_send, edge_recv, row_send, row_recv, fold_send, fold_recv, rim_send, rim_recv, sum_send, sum_recv, line_sem,
):
    ext = (ext_first, ext_second)
    slots = intensity.shape[0]
    row, col = lax.axis_index("row"), lax.axis_index("col")
    up, down = lax.rem(row + rows - 1, rows), lax.rem(row + 1, rows)
    left, right = lax.rem(col + cols - 1, cols), lax.rem(col + 1, cols)
    lane = lax.broadcasted_iota(jnp.int32, (HALF, SIDE), 1)
    low = lane < HALF
    own = slice(HALF, 2 * HALF)

    own_loads = [
        [
            pltpu.make_async_copy(
                trans.at[:, layer, :, pl.ds(tile * SIDE, SIDE)], ext[layer].at[:, tile, own, :], load_sem.at[layer * 2 + tile]
            )
            for tile in range(2)
        ]
        for layer in range(2)
    ]
    small_loads = [
        pltpu.make_async_copy(src, dst, load_sem.at[4 + i])
        for i, (src, dst) in enumerate(
            [(phase_in, phase), (probe_in, probe), (intensity_in, intensity)]
        )
    ]
    for layer in own_loads:
        for copy in layer:
            copy.start()
    for copy in small_loads:
        copy.start()

    x_side, line = rows // (2 * Z_LOW), Z_LOW * (cols // Y_SIDE)
    plane = x_side * Y_SIDE
    x, z_low, core = lax.div(row, 2 * Z_LOW), lax.rem(lax.div(row, 2), Z_LOW), lax.rem(row, 2)
    y, z = lax.rem(col, Y_SIDE), lax.div(col, Y_SIDE) * Z_LOW + z_low
    spot_in_plane = x * Y_SIDE + y

    def plane_peer(k):
        to_x = lax.rem(x + lax.div(k, Y_SIDE), x_side)
        to_y = lax.rem(y + lax.rem(k, Y_SIDE), Y_SIDE)
        return to_x * Y_SIDE + to_y, {"row": (to_x * Z_LOW + z_low) * 2 + core, "col": col - y + to_y}

    def line_peer(k):
        to_z = lax.rem(z + k, line)
        return {"row": (x * Z_LOW + lax.rem(to_z, Z_LOW)) * 2 + core, "col": lax.div(to_z, Z_LOW) * Y_SIDE + y}

    def across(device):
        return {**device, "row": device["row"] + 1 - 2 * core}

    sibling = across({"row": row, "col": col})

    barrier = pltpu.get_barrier_semaphore()

    def greet(device):
        pl.semaphore_signal(barrier, inc=1, device_id=device, device_id_type=MESH)

    def greet_plane(k, _):
        greet(plane_peer(k)[1])
        greet(across(plane_peer(k)[1]))
        return 0

    for device in ({"row": up}, {"row": down}, {"col": left}, {"col": right}, line_peer(1), line_peer(line - 1)):
        greet(device)
    lax.fori_loop(1, plane, greet_plane, 0)

    reaches = []
    while 2 ** len(reaches) < line // 2:
        reaches.append(2 ** len(reaches))

    def line_signal(turn):
        if turn < len(reaches):
            for k in (reaches[turn], line - reaches[turn]):
                pl.semaphore_signal(line_sem.at[turn], inc=1, device_id=line_peer(k), device_id_type=MESH)

    def line_wait(turn):
        if turn < len(reaches):
            pl.semaphore_wait(line_sem.at[turn], 2)

    def edge_copies(layer):
        return [
            remote(edge_out.at[layer, 0], edge_in.at[layer, 0], edge_send.at[layer, 0], edge_recv.at[layer, 0], {"col": right}),
            remote(edge_out.at[layer, 1], edge_in.at[layer, 1], edge_send.at[layer, 1], edge_recv.at[layer, 1], {"col": left}),
        ]

    def row_copies(layer, part):
        tiles = slice(0, 2) if part == 0 else slice(2, 3)
        src = ext[layer].at[:, tiles, own, :]
        return [
            remote(
                src, ext[layer].at[:, tiles, 0:HALF, :],
                row_send.at[layer, part, 0], row_recv.at[layer, part, 0], {"row": down},
            ),
            remote(
                src, ext[layer].at[:, tiles, 2 * HALF : 3 * HALF, :],
                row_send.at[layer, part, 1], row_recv.at[layer, part, 1], {"row": up},
            ),
        ]

    def start(copies):
        for copy in copies:
            copy.start()

    def landed(copies):
        for copy in copies:
            copy.wait_recv()

    def sent(copies):
        for copy in copies:
            copy.wait_send()

    for layer in range(2):
        for copy in own_loads[layer]:
            copy.wait()
        edge_out[layer, 0] = jnp.where(
            low, pltpu.roll(ext[layer][1, 1, own, :], HALF, 1), ext[layer][0, 1, own, :]
        )
        edge_out[layer, 1] = jnp.where(
            low, ext[layer][0, 0, own, :], pltpu.roll(ext[layer][1, 0, own, :], HALF, 1)
        )
    pl.semaphore_wait(barrier, 2 * (plane - 1) + 6)
    start(edge_copies(0))
    start(row_copies(0, 0))
    start(edge_copies(1))
    line_signal(0)

    for i, table in enumerate(dft_tables()):
        tables[2 * i], tables[2 * i + 1] = halves(table)
    for copy in small_loads:
        copy.wait()
    prop[0] = jnp.cos(phase[...])
    prop[1] = jnp.sin(phase[...])
    place[:, :, :, 0:2, 0:HALF, :] = jnp.zeros(place.shape[:3] + (2, HALF, SIDE), jnp.float32)
    place[:, :, :, 0:2, 3 * HALF :, :] = jnp.zeros(place.shape[:3] + (2, HALF, SIDE), jnp.float32)
    place[:, :, :, 2, :, :] = jnp.zeros(place.shape[:3] + (4 * HALF, SIDE), jnp.float32)
    line_wait(0)
    line_signal(1)

    for layer in range(2):
        landed(edge_copies(layer))
        from_left = jnp.where(col > 0, edge_in[layer, 0], 0.0)
        from_right = jnp.where(col < cols - 1, edge_in[layer, 1], 0.0)
        ext[layer][0, 2, own, :] = jnp.where(low, from_right, from_left)
        ext[layer][1, 2, own, :] = pltpu.roll(jnp.where(low, from_left, from_right), HALF, 1)
        start(row_copies(layer, 1))
        if layer == 0:
            start(row_copies(1, 0))
    line_wait(1)
    line_signal(2)

    lanes = lax.broadcasted_iota(jnp.int32, (SIDE, SIDE), 1)

    def spot(slot):
        across = offsets[1, slot] + (TILES * SIDE - HALF)
        tile = lax.rem(lax.div(across, SIDE), TILES)
        return offsets[0, slot], tile, lax.rem(tile + 1, TILES), lax.rem(across, SIDE)

    spots = [spot(slot) for slot in range(slots)]

    def rows_arrived(layer):
        landed(row_copies(layer, 0))
        landed(row_copies(layer, 1))

        @pl.when(row == 0)
        def _():
            ext[layer][:, :, 0:HALF, :] = jnp.zeros((2, TILES, HALF, SIDE), jnp.float32)

        @pl.when(row == rows - 1)
        def _():
            ext[layer][:, :, 2 * HALF :, :] = jnp.zeros((2, TILES, HALF, SIDE), jnp.float32)

    def gather(layer):
        for slot, (top, tile, after, shift) in enumerate(spots):
            back = lax.rem(SIDE - shift, SIDE)
            for part in range(2):
                first = ext[layer][part, tile, pl.ds(top, SIDE), :]
                second = ext[layer][part, after, pl.ds(top, SIDE), :]
                patch[layer, part, slot * SIDE : (slot + 1) * SIDE, :] = pltpu.roll(
                    jnp.where(lanes < shift, second, first), back, 1
                )

    def scatter(layer, grad):
        for slot, (_, _, _, shift) in enumerate(spots):
            for part in range(2):
                moved = pltpu.roll(grad[part][slot * SIDE : (slot + 1) * SIDE], shift, 1)
                place[layer, part, slot, 0, HALF : 3 * HALF, :] = jnp.where(lanes < shift, 0.0, moved)
                place[layer, part, slot, 1, HALF : 3 * HALF, :] = jnp.where(lanes < shift, moved, 0.0)
        for tile in reversed(range(TILES)):
            for part in range(2):
                total = None
                for slot, (top, first, second, _) in enumerate(spots):
                    which = jnp.where(first == tile, 0, jnp.where(second == tile, 1, 2))
                    term = place[layer, part, slot, which, pl.ds(HALF - top, 3 * HALF), :]
                    total = term if total is None else total + term
                grid[layer, part, tile] = total
            if tile == 2:
                start(fold_copies(layer, 1))
        if layer == 1:
            start(fold_copies(layer, 0))

    def fold_copies(layer, part):
        tiles = slice(0, 2) if part == 0 else slice(2, 3)
        return [
            remote(
                grid.at[layer, :, tiles, 2 * HALF : 3 * HALF, :], fold_in.at[layer, 0, :, tiles],
                fold_send.at[layer, part, 0], fold_recv.at[layer, part, 0], {"row": down},
            ),
            remote(
                grid.at[layer, :, tiles, 0:HALF, :], fold_in.at[layer, 1, :, tiles],
                fold_send.at[layer, part, 1], fold_recv.at[layer, part, 1], {"row": up},
            ),
        ]

    def rim_copies(layer):
        return [
            remote(rim_out.at[layer, 0], rim_in.at[layer, 0], rim_send.at[layer, 0], rim_recv.at[layer, 0], {"col": right}),
            remote(rim_out.at[layer, 1], rim_in.at[layer, 1], rim_send.at[layer, 1], rim_recv.at[layer, 1], {"col": left}),
        ]

    repeat = lambda part: jnp.concatenate([part] * slots, axis=0)
    wide = (tables[0], tables[1])
    tall = (tables[2], tables[3])

    def transform(field):
        return along_rows(*along_lanes(*field, wide), tall)

    def inverse(field):
        return along_rows(*along_lanes(*field, tall), wide)

    shone = (repeat(probe[0]), repeat(probe[1]))
    moved = (repeat(prop[0]), repeat(prop[1]))

    rows_arrived(0)
    gather(0)
    field = times(*shone, patch[0, 0], patch[0, 1])
    field = inverse(times(*transform(field), *moved))
    wave[0] = field[0]
    wave[1] = field[1]
    rows_arrived(1)
    gather(1)
    far = transform(times(*field, patch[1, 0], patch[1, 1]))
    live = jnp.concatenate(
        [jnp.full((SIDE, SIDE), jnp.where(slot < counts[0], 2.0, 0.0), jnp.float32) for slot in range(slots)], axis=0
    )
    measured = jnp.concatenate([intensity[slot].astype(jnp.float32) for slot in range(slots)], axis=0)
    excess = (far[0] * far[0] + far[1] * far[1] - measured) * live
    back = inverse((far[0] * excess, far[1] * excess))
    scatter(1, times_conj(*back, wave[0], wave[1]))
    back = transform(times_conj(*back, patch[1, 0], patch[1, 1]))
    back = inverse(times_conj(*back, *moved))
    probe_grad = times_conj(*back, patch[0, 0], patch[0, 1])

    scale = 1.0 / math.sqrt(total_slots)
    for part in range(2):
        acc = probe_grad[part][:SIDE]
        for slot in range(1, slots):
            acc = acc + probe_grad[part][slot * SIDE : (slot + 1) * SIDE]
        sum_out[part] = acc * scale

    def wait_bytes(ref, sem):
        pltpu.make_async_copy(ref, ref, sem).wait()

    hops = lambda k, count: min(k, count - k)
    line_order = sorted(range(1, line), key=lambda k: -hops(k, line))
    plane_order = sorted(range(1, plane), key=lambda k: -hops(k // Y_SIDE, x_side) - hops(k % Y_SIDE, Y_SIDE))

    def start_all(copy, order):
        for k in order:
            copy(k).start()

    halves_in = remote(sum_out.at[1 - core], core_in, sum_send.at[0], sum_recv.at[0], sibling)

    def scatter_piece(k):
        index, device = plane_peer(k)
        return remote(plane_out.at[index], plane_in.at[spot_in_plane], sum_send.at[1], sum_recv.at[1], device)

    def share_piece(k):
        return remote(line_in.at[z], line_in.at[z], sum_send.at[2], sum_recv.at[2], line_peer(k))

    def spread_piece(k):
        mine = gathered.at[core, spot_in_plane]
        return remote(mine, mine, sum_send.at[3], sum_recv.at[3], plane_peer(k)[1])

    def spread_across(k):
        mine = gathered.at[core, spot_in_plane]
        return remote(mine, mine, sum_send.at[4], sum_recv.at[4], across(plane_peer(k)[1]))

    def fold(layer, tile, part):
        above = jnp.where(row > 0, fold_in[layer, 0, part, tile], 0.0)
        below = jnp.where(row < rows - 1, fold_in[layer, 1, part, tile], 0.0)
        return grid[layer, part, tile, own, :] + above + below

    def fold_rims(layer):
        landed(fold_copies(layer, 1))
        re, im = fold(layer, 2, 0), fold(layer, 2, 1)
        turned = pltpu.roll(im, HALF, 1)
        rim_out[layer, 0] = jnp.where(low, re, turned)
        rim_out[layer, 1] = jnp.where(low, turned, re)
        start(rim_copies(layer))

    def fold_tiles(layer):
        landed(fold_copies(layer, 0))
        landed(rim_copies(layer))
        from_left = jnp.where(col > 0, rim_in[layer, 0], 0.0)
        from_right = jnp.where(col < cols - 1, rim_in[layer, 1], 0.0)
        for part in range(2):
            if part == 1:
                from_left, from_right = pltpu.roll(from_left, HALF, 1), pltpu.roll(from_right, HALF, 1)
            object_out[part, layer, :, 0:SIDE] = fold(layer, 0, part) + jnp.where(low, from_left, 0.0)
            object_out[part, layer, :, SIDE:] = fold(layer, 1, part) + jnp.where(low, 0.0, from_right)

    halves_in.start()
    scatter(0, times_conj(*back, *shone))
    halves_in.wait_recv()
    plane_out[...] = (sum_out[core] + core_in[...]).reshape(plane_out.shape)
    start_all(scatter_piece, plane_order)
    fold_rims(1)
    plane_in[spot_in_plane] = plane_out[spot_in_plane]
    wait_bytes(plane_in.at[pl.ds(0, plane - 1)], sum_recv.at[1])
    line_in[z] = jnp.sum(plane_in[...], axis=0)
    line_wait(2)
    start_all(share_piece, line_order)
    start(fold_copies(0, 0))
    fold_rims(0)
    fold_tiles(1)
    wait_bytes(line_in.at[pl.ds(0, line - 1)], sum_recv.at[2])
    gathered[core, spot_in_plane] = jnp.sum(line_in[...], axis=0)
    start_all(spread_piece, plane_order)
    start_all(spread_across, plane_order + [0])
    fold_tiles(0)
    pieces = gathered.at[core, pl.ds(0, plane - 1)]
    wait_bytes(pieces, sum_recv.at[3])
    halves_in.wait_send()
    wait_bytes(plane_in.at[pl.ds(0, plane - 1)], sum_send.at[1])
    wait_bytes(line_in.at[pl.ds(0, line - 1)], sum_send.at[2])
    wait_bytes(pieces, sum_send.at[3])
    for layer in range(2):
        sent(edge_copies(layer))
        sent(rim_copies(layer))
        for part in range(2):
            sent(row_copies(layer, part))
            sent(fold_copies(layer, part))
    wait_bytes(gathered.at[1 - core], sum_recv.at[4])
    wait_bytes(gathered.at[1 - core], sum_send.at[4])
    probe_out[...] = gathered[...].reshape(probe_out.shape)


def solution(mesh):
    rows, cols = mesh.shape["row"], mesh.shape["col"]

    def shards(transmission, probe, prop_phase, intensity, offsets, counts):
        slots = offsets.shape[0]
        f32 = jnp.float32
        plane = rows // (2 * Z_LOW) * Y_SIDE
        line = Z_LOW * (cols // Y_SIDE)
        depth = SIDE // plane
        hbm = pl.BlockSpec(memory_space=pltpu.HBM)
        smem = pl.BlockSpec(memory_space=pltpu.SMEM)
        vmem = pl.BlockSpec(memory_space=pltpu.VMEM)
        dma = pltpu.SemaphoreType.DMA
        return pl.pallas_call(
            functools.partial(kernel, rows, cols, slots * rows * cols),
            out_shape=(
                jax.ShapeDtypeStruct(transmission.shape, f32),
                jax.ShapeDtypeStruct(probe.shape, f32),
            ),
            in_specs=[smem, smem] + [hbm] * 4,
            out_specs=(vmem, vmem),
            scratch_shapes=[
                pltpu.VMEM((2, TILES, 3 * HALF, SIDE), f32),
                pltpu.VMEM((2, TILES, 3 * HALF, SIDE), f32),
                pltpu.VMEM(probe.shape, f32),
                pltpu.VMEM(prop_phase.shape, f32),
                pltpu.VMEM(intensity.shape, intensity.dtype),
                pltpu.VMEM((4, 2 * SIDE, 2 * SIDE), jnp.bfloat16),
                pltpu.VMEM((2, 2, HALF, SIDE), f32),
                pltpu.VMEM((2, 2, HALF, SIDE), f32),
                pltpu.VMEM((2, 2, slots * SIDE, SIDE), f32),
                pltpu.VMEM((2, slots * SIDE, SIDE), f32),
                pltpu.VMEM((2, SIDE, SIDE), f32),
                pltpu.VMEM((2, 2, slots, 3, 4 * HALF, SIDE), f32),
                pltpu.VMEM((2, 2, TILES, 3 * HALF, SIDE), f32),
                pltpu.VMEM((2, 2, 2, TILES, HALF, SIDE), f32),
                pltpu.VMEM((2, 2, HALF, SIDE), f32),
                pltpu.VMEM((2, 2, HALF, SIDE), f32),
                pltpu.VMEM((2, SIDE, SIDE), f32),
                pltpu.VMEM((SIDE, SIDE), f32),
                pltpu.VMEM((plane, depth, SIDE), f32),
                pltpu.VMEM((plane, depth, SIDE), f32),
                pltpu.VMEM((line, depth, SIDE), f32),
                pltpu.VMEM((2, plane, depth, SIDE), f32),
                dma((7,)),
                dma((2, 2)),
                dma((2, 2)),
                dma((2, 2, 2)),
                dma((2, 2, 2)),
                dma((2, 2, 2)),
                dma((2, 2, 2)),
                dma((2, 2)),
                dma((2, 2)),
                dma((5,)),
                dma((5,)),
                pltpu.SemaphoreType.REGULAR((3,)),
            ],
            compiler_params=pltpu.CompilerParams(
                collective_id=0, has_side_effects=True, vmem_limit_bytes=60 * 1024 * 1024
            ),
        )(offsets.T, counts, transmission, probe, prop_phase, intensity)

    in_specs = (
        P(None, None, "row", "col"),
        P(),
        P(),
        P(("row", "col"), None, None),
        P(("row", "col"), None),
        P(("row", "col")),
    )
    out_specs = (P(None, None, "row", "col"), P())
    return jax.shard_map(shards, mesh=mesh, in_specs=in_specs, out_specs=out_specs, check_vma=False)
```

```python
import functools
import math

import jax
import jax.numpy as jnp
from jax import lax
from jax.experimental import pallas as pl
from jax.experimental.pallas import tpu as pltpu
from jax.sharding import PartitionSpec as P

MESH = pl.DeviceIdType.MESH
SIDE = 128
HALF = 64
TILES = 3
Z_LOW = 4
Y_SIDE = 4


def dft_tables():
    rows = lax.broadcasted_iota(jnp.int32, (SIDE, SIDE), 0)
    lanes = lax.broadcasted_iota(jnp.int32, (SIDE, SIDE), 1)
    angles = lax.rem(rows * lanes, SIDE).astype(jnp.float32) * (-2.0 * math.pi / SIDE)
    re, im = jnp.cos(angles) * (1.0 / math.sqrt(SIDE)), jnp.sin(angles) * (1.0 / math.sqrt(SIDE))
    block = lambda a, b, c, d: jnp.concatenate(
        [jnp.concatenate([a, b], axis=1), jnp.concatenate([c, d], axis=1)], axis=0
    )
    return block(re, im, -im, re), block(re, -im, im, re)


def halves(value):
    high = value.astype(jnp.bfloat16)
    return high, (value - high.astype(jnp.float32)).astype(jnp.bfloat16)


def product(left, right):
    dot = functools.partial(jnp.dot, preferred_element_type=jnp.float32)
    return dot(left[0], right[0]) + dot(left[1], right[0]) + dot(left[0], right[1])


def along_lanes(re, im, table):
    out = product(halves(jnp.concatenate([re, im], axis=1)), table)
    return out[:, :SIDE], out[:, SIDE:]


def along_rows(re, im, table):
    slots = re.shape[0] // SIDE
    beside = lambda part: jnp.concatenate([part[s * SIDE : (s + 1) * SIDE] for s in range(slots)], axis=1)
    out = product(table, halves(jnp.concatenate([beside(re), beside(im)], axis=0)))
    below = lambda part: jnp.concatenate([part[:, s * SIDE : (s + 1) * SIDE] for s in range(slots)], axis=0)
    return below(out[:SIDE]), below(out[SIDE:])


def times(a_re, a_im, b_re, b_im):
    return a_re * b_re - a_im * b_im, a_re * b_im + a_im * b_re


def times_conj(a_re, a_im, b_re, b_im):
    return a_re * b_re + a_im * b_im, a_im * b_re - a_re * b_im


def remote(src, dst, send, recv, device):
    return pltpu.make_async_remote_copy(
        src_ref=src, dst_ref=dst, send_sem=send, recv_sem=recv, device_id=device, device_id_type=MESH
    )


def kernel(
    rows, cols, total_slots,
    offsets, counts, trans, probe_in, phase_in, intensity_in,
    object_out, probe_out,
    ext_first, ext_second, relay_in, probe, phase, intensity, tables, edge_out, edge_in, patch, wave, prop, place, grid, fold_in, rim_out, rim_in,
    sum_out, core_in, plane_out, plane_in, line_in, gathered,
    load_sem, edge_send, edge_recv, row_send, row_recv, fold_send, fold_recv, rim_send, rim_recv, sum_send, sum_recv, line_sem, relay_send, relay_recv,
):
    ext = (ext_first, ext_second)
    slots = intensity.shape[0]
    row, col = lax.axis_index("row"), lax.axis_index("col")
    up, down = lax.rem(row + rows - 1, rows), lax.rem(row + 1, rows)
    left, right = lax.rem(col + cols - 1, cols), lax.rem(col + 1, cols)
    lane = lax.broadcasted_iota(jnp.int32, (HALF, SIDE), 1)
    low = lane < HALF
    own = slice(HALF, 2 * HALF)

    own_loads = [
        [
            pltpu.make_async_copy(
                trans.at[:, layer, :, pl.ds(tile * SIDE, SIDE)], ext[layer].at[:, tile, own, :], load_sem.at[layer * 2 + tile]
            )
            for tile in range(2)
        ]
        for layer in range(2)
    ]
    small_loads = [
        pltpu.make_async_copy(src, dst, load_sem.at[4 + i])
        for i, (src, dst) in enumerate(
            [(phase_in, phase), (probe_in, probe), (intensity_in, intensity)]
        )
    ]
    for layer in own_loads:
        for copy in layer:
            copy.start()
    for copy in small_loads:
        copy.start()

    x_side, line = rows // (2 * Z_LOW), Z_LOW * (cols // Y_SIDE)
    plane = x_side * Y_SIDE
    x, z_low, core = lax.div(row, 2 * Z_LOW), lax.rem(lax.div(row, 2), Z_LOW), lax.rem(row, 2)
    y, z = lax.rem(col, Y_SIDE), lax.div(col, Y_SIDE) * Z_LOW + z_low
    spot_in_plane = x * Y_SIDE + y

    def plane_peer(k):
        to_x = lax.rem(x + lax.div(k, Y_SIDE), x_side)
        to_y = lax.rem(y + lax.rem(k, Y_SIDE), Y_SIDE)
        return to_x * Y_SIDE + to_y, {"row": (to_x * Z_LOW + z_low) * 2 + core, "col": col - y + to_y}

    def line_peer(k):
        to_z = lax.rem(z + k, line)
        return {"row": (x * Z_LOW + lax.rem(to_z, Z_LOW)) * 2 + core, "col": lax.div(to_z, Z_LOW) * Y_SIDE + y}

    def across(device):
        return {**device, "row": device["row"] + 1 - 2 * core}

    sibling = across({"row": row, "col": col})

    barrier = pltpu.get_barrier_semaphore()

    def greet(device):
        pl.semaphore_signal(barrier, inc=1, device_id=device, device_id_type=MESH)

    def greet_plane(k, _):
        greet(plane_peer(k)[1])
        greet(across(plane_peer(k)[1]))
        return 0

    for device in ({"row": up}, {"row": down}, {"col": left}, {"col": right}, line_peer(1), line_peer(line - 1)):
        greet(device)
    lax.fori_loop(1, plane, greet_plane, 0)

    reaches = []
    while 2 ** len(reaches) < line // 2:
        reaches.append(2 ** len(reaches))

    def line_signal(turn):
        if turn < len(reaches):
            for k in (reaches[turn], line - reaches[turn]):
                pl.semaphore_signal(line_sem.at[turn], inc=1, device_id=line_peer(k), device_id_type=MESH)

    def line_wait(turn):
        if turn < len(reaches):
            pl.semaphore_wait(line_sem.at[turn], 2)

    def edge_copies(layer):
        return [
            remote(edge_out.at[layer, 0], edge_in.at[layer, 0], edge_send.at[layer, 0], edge_recv.at[layer, 0], {"col": right}),
            remote(edge_out.at[layer, 1], edge_in.at[layer, 1], edge_send.at[layer, 1], edge_recv.at[layer, 1], {"col": left}),
        ]

    def row_copies(layer, part):
        tiles = slice(0, 2) if part == 0 else slice(2, 3)
        src = ext[layer].at[:, tiles, own, :]
        return [
            remote(
                src, ext[layer].at[:, tiles, 0:HALF, :],
                row_send.at[layer, part, 0], row_recv.at[layer, part, 0], {"row": down},
            ),
            remote(
                src, ext[layer].at[:, tiles, 2 * HALF : 3 * HALF, :],
                row_send.at[layer, part, 1], row_recv.at[layer, part, 1], {"row": up},
            ),
        ]

    depth = HALF // Y_SIDE
    part_rows = lambda k: pl.ds(pl.multiple_of(k * depth, depth), depth)
    seams = ((Y_SIDE - 1, 1, lax.rem(col - y + Y_SIDE, cols)), (0, -1, lax.rem(col - y - 1 + cols, cols)))

    def start_spread(turn, copies, out, into, send, recv):
        for way, (seam, step, _) in enumerate(seams):

            @pl.when(y != seam)
            def _(way=way):
                copies[way].start()

            @pl.when(y == seam)
            def _(way=way, seam=seam, step=step):
                for k in range(1, Y_SIDE):
                    device = {"col": col - y + (seam + step * k) % Y_SIDE}
                    remote(
                        out.at[way, part_rows(k)], relay_in.at[turn, way], send.at[way], relay_recv.at[turn, way], device
                    ).start()
                beyond = {"col": right if way == 0 else left}
                remote(out.at[way, part_rows(0)], into.at[way, part_rows(0)], send.at[way], recv.at[way], beyond).start()

    def relayed(turn, way, into, recv):
        seam, _, beyond = seams[way]
        k = y + 1 if way == 0 else lax.rem(Y_SIDE - y, Y_SIDE)
        k = lax.rem(k, Y_SIDE)
        return remote(
            relay_in.at[turn, way], into.at[way, part_rows(k)], relay_send.at[turn, way], recv.at[way], {"col": beyond}
        )

    def relay(turn, into, recv):
        for way, (seam, _, _) in enumerate(seams):

            @pl.when(y != seam)
            def _(way=way):
                here = relay_in.at[turn, way]
                pltpu.make_async_copy(here, here, relay_recv.at[turn, way]).wait()
                relayed(turn, way, into, recv).start()

    def relay_done(turn, into, recv):
        for way, (seam, _, _) in enumerate(seams):

            @pl.when(y != seam)
            def _(way=way):
                relayed(turn, way, into, recv).wait_send()

    edge_refs = lambda layer: (edge_out.at[layer], edge_in.at[layer], edge_send.at[layer], edge_recv.at[layer])
    rim_refs = lambda layer: (rim_out.at[layer], rim_in.at[layer], rim_send.at[layer], rim_recv.at[layer])

    def start(copies):
        for copy in copies:
            copy.start()

    def landed(copies):
        for copy in copies:
            copy.wait_recv()

    def sent(copies):
        for copy in copies:
            copy.wait_send()

    for layer in range(2):
        for copy in own_loads[layer]:
            copy.wait()
        edge_out[layer, 0] = jnp.where(
            low, pltpu.roll(ext[layer][1, 1, own, :], HALF, 1), ext[layer][0, 1, own, :]
        )
        edge_out[layer, 1] = jnp.where(
            low, ext[layer][0, 0, own, :], pltpu.roll(ext[layer][1, 0, own, :], HALF, 1)
        )
    pl.semaphore_wait(barrier, 2 * (plane - 1) + 6)
    start(edge_copies(0))
    start_spread(0, edge_copies(1), *edge_refs(1))
    start(row_copies(0, 0))
    line_signal(0)

    for i, table in enumerate(dft_tables()):
        tables[2 * i], tables[2 * i + 1] = halves(table)
    for copy in small_loads:
        copy.wait()
    prop[0] = jnp.cos(phase[...])
    prop[1] = jnp.sin(phase[...])
    place[:, :, :, 0:2, 0:HALF, :] = jnp.zeros(place.shape[:3] + (2, HALF, SIDE), jnp.float32)
    place[:, :, :, 0:2, 3 * HALF :, :] = jnp.zeros(place.shape[:3] + (2, HALF, SIDE), jnp.float32)
    place[:, :, :, 2, :, :] = jnp.zeros(place.shape[:3] + (4 * HALF, SIDE), jnp.float32)
    relay(0, *edge_refs(1)[1::2])
    line_wait(0)
    line_signal(1)

    for layer in range(2):
        landed(edge_copies(layer))
        from_left = jnp.where(col > 0, edge_in[layer, 0], 0.0)
        from_right = jnp.where(col < cols - 1, edge_in[layer, 1], 0.0)
        ext[layer][0, 2, own, :] = jnp.where(low, from_right, from_left)
        ext[layer][1, 2, own, :] = pltpu.roll(jnp.where(low, from_left, from_right), HALF, 1)
        start(row_copies(layer, 1))
        if layer == 0:
            start(row_copies(1, 0))
    line_wait(1)
    line_signal(2)

    lanes = lax.broadcasted_iota(jnp.int32, (SIDE, SIDE), 1)

    def spot(slot):
        across = offsets[1, slot] + (TILES * SIDE - HALF)
        tile = lax.rem(lax.div(across, SIDE), TILES)
        return offsets[0, slot], tile, lax.rem(tile + 1, TILES), lax.rem(across, SIDE)

    spots = [spot(slot) for slot in range(slots)]

    def rows_arrived(layer):
        landed(row_copies(layer, 0))
        landed(row_copies(layer, 1))

        @pl.when(row == 0)
        def _():
            ext[layer][:, :, 0:HALF, :] = jnp.zeros((2, TILES, HALF, SIDE), jnp.float32)

        @pl.when(row == rows - 1)
        def _():
            ext[layer][:, :, 2 * HALF :, :] = jnp.zeros((2, TILES, HALF, SIDE), jnp.float32)

    def gather(layer):
        for slot, (top, tile, after, shift) in enumerate(spots):
            back = lax.rem(SIDE - shift, SIDE)
            for part in range(2):
                first = ext[layer][part, tile, pl.ds(top, SIDE), :]
                second = ext[layer][part, after, pl.ds(top, SIDE), :]
                patch[layer, part, slot * SIDE : (slot + 1) * SIDE, :] = pltpu.roll(
                    jnp.where(lanes < shift, second, first), back, 1
                )

    def scatter(layer, grad):
        for slot, (_, _, _, shift) in enumerate(spots):
            for part in range(2):
                moved = pltpu.roll(grad[part][slot * SIDE : (slot + 1) * SIDE], shift, 1)
                place[layer, part, slot, 0, HALF : 3 * HALF, :] = jnp.where(lanes < shift, 0.0, moved)
                place[layer, part, slot, 1, HALF : 3 * HALF, :] = jnp.where(lanes < shift, moved, 0.0)
        for tile in reversed(range(TILES)):
            for part in range(2):
                total = None
                for slot, (top, first, second, _) in enumerate(spots):
                    which = jnp.where(first == tile, 0, jnp.where(second == tile, 1, 2))
                    term = place[layer, part, slot, which, pl.ds(HALF - top, 3 * HALF), :]
                    total = term if total is None else total + term
                grid[layer, part, tile] = total
            if tile == 2:
                start(fold_copies(layer, 1))
        if layer == 1:
            start(fold_copies(layer, 0))

    def fold_copies(layer, part):
        tiles = slice(0, 2) if part == 0 else slice(2, 3)
        return [
            remote(
                grid.at[layer, :, tiles, 2 * HALF : 3 * HALF, :], fold_in.at[layer, 0, :, tiles],
                fold_send.at[layer, part, 0], fold_recv.at[layer, part, 0], {"row": down},
            ),
            remote(
                grid.at[layer, :, tiles, 0:HALF, :], fold_in.at[layer, 1, :, tiles],
                fold_send.at[layer, part, 1], fold_recv.at[layer, part, 1], {"row": up},
            ),
        ]

    def rim_copies(layer):
        return [
            remote(rim_out.at[layer, 0], rim_in.at[layer, 0], rim_send.at[layer, 0], rim_recv.at[layer, 0], {"col": right}),
            remote(rim_out.at[layer, 1], rim_in.at[layer, 1], rim_send.at[layer, 1], rim_recv.at[layer, 1], {"col": left}),
        ]

    repeat = lambda part: jnp.concatenate([part] * slots, axis=0)
    wide = (tables[0], tables[1])
    tall = (tables[2], tables[3])

    def transform(field):
        return along_rows(*along_lanes(*field, wide), tall)

    def inverse(field):
        return along_rows(*along_lanes(*field, tall), wide)

    shone = (repeat(probe[0]), repeat(probe[1]))
    moved = (repeat(prop[0]), repeat(prop[1]))

    rows_arrived(0)
    gather(0)
    field = times(*shone, patch[0, 0], patch[0, 1])
    field = inverse(times(*transform(field), *moved))
    wave[0] = field[0]
    wave[1] = field[1]
    rows_arrived(1)
    gather(1)
    far = transform(times(*field, patch[1, 0], patch[1, 1]))
    live = jnp.concatenate(
        [jnp.full((SIDE, SIDE), jnp.where(slot < counts[0], 2.0, 0.0), jnp.float32) for slot in range(slots)], axis=0
    )
    measured = jnp.concatenate([intensity[slot].astype(jnp.float32) for slot in range(slots)], axis=0)
    excess = (far[0] * far[0] + far[1] * far[1] - measured) * live
    back = inverse((far[0] * excess, far[1] * excess))
    scatter(1, times_conj(*back, wave[0], wave[1]))
    back = transform(times_conj(*back, patch[1, 0], patch[1, 1]))
    back = inverse(times_conj(*back, *moved))
    probe_grad = times_conj(*back, patch[0, 0], patch[0, 1])

    scale = 1.0 / math.sqrt(total_slots)
    for part in range(2):
        acc = probe_grad[part][:SIDE]
        for slot in range(1, slots):
            acc = acc + probe_grad[part][slot * SIDE : (slot + 1) * SIDE]
        sum_out[part] = acc * scale

    def wait_bytes(ref, sem):
        pltpu.make_async_copy(ref, ref, sem).wait()

    hops = lambda k, count: min(k, count - k)
    line_order = sorted(range(1, line), key=lambda k: -hops(k, line))
    plane_order = sorted(range(1, plane), key=lambda k: -hops(k // Y_SIDE, x_side) - hops(k % Y_SIDE, Y_SIDE))

    def start_all(copy, order):
        for k in order:
            copy(k).start()

    halves_in = remote(sum_out.at[1 - core], core_in, sum_send.at[0], sum_recv.at[0], sibling)

    def scatter_piece(k):
        index, device = plane_peer(k)
        return remote(plane_out.at[index], plane_in.at[spot_in_plane], sum_send.at[1], sum_recv.at[1], device)

    def share_piece(k):
        return remote(line_in.at[z], line_in.at[z], sum_send.at[2], sum_recv.at[2], line_peer(k))

    def spread_piece(k):
        mine = gathered.at[core, spot_in_plane]
        return remote(mine, mine, sum_send.at[3], sum_recv.at[3], plane_peer(k)[1])

    def spread_across(k):
        mine = gathered.at[core, spot_in_plane]
        return remote(mine, mine, sum_send.at[4], sum_recv.at[4], across(plane_peer(k)[1]))

    def fold(layer, tile, part):
        above = jnp.where(row > 0, fold_in[layer, 0, part, tile], 0.0)
        below = jnp.where(row < rows - 1, fold_in[layer, 1, part, tile], 0.0)
        return grid[layer, part, tile, own, :] + above + below

    def fold_rims(layer):
        landed(fold_copies(layer, 1))
        re, im = fold(layer, 2, 0), fold(layer, 2, 1)
        turned = pltpu.roll(im, HALF, 1)
        rim_out[layer, 0] = jnp.where(low, re, turned)
        rim_out[layer, 1] = jnp.where(low, turned, re)
        start_spread(2 - layer, rim_copies(layer), *rim_refs(layer))

    def fold_tiles(layer):
        landed(fold_copies(layer, 0))
        landed(rim_copies(layer))
        from_left = jnp.where(col > 0, rim_in[layer, 0], 0.0)
        from_right = jnp.where(col < cols - 1, rim_in[layer, 1], 0.0)
        for part in range(2):
            if part == 1:
                from_left, from_right = pltpu.roll(from_left, HALF, 1), pltpu.roll(from_right, HALF, 1)
            object_out[part, layer, :, 0:SIDE] = fold(layer, 0, part) + jnp.where(low, from_left, 0.0)
            object_out[part, layer, :, SIDE:] = fold(layer, 1, part) + jnp.where(low, 0.0, from_right)

    halves_in.start()
    scatter(0, times_conj(*back, *shone))
    halves_in.wait_recv()
    plane_out[...] = (sum_out[core] + core_in[...]).reshape(plane_out.shape)
    start_all(scatter_piece, plane_order)
    fold_rims(1)
    relay(1, *rim_refs(1)[1::2])
    plane_in[spot_in_plane] = plane_out[spot_in_plane]
    wait_bytes(plane_in.at[pl.ds(0, plane - 1)], sum_recv.at[1])
    line_in[z] = jnp.sum(plane_in[...], axis=0)
    line_wait(2)
    start_all(share_piece, line_order)
    start(fold_copies(0, 0))
    fold_rims(0)
    fold_tiles(1)
    relay(2, *rim_refs(0)[1::2])
    wait_bytes(line_in.at[pl.ds(0, line - 1)], sum_recv.at[2])
    gathered[core, spot_in_plane] = jnp.sum(line_in[...], axis=0)
    start_all(spread_piece, plane_order)
    start_all(spread_across, plane_order + [0])
    fold_tiles(0)
    pieces = gathered.at[core, pl.ds(0, plane - 1)]
    wait_bytes(pieces, sum_recv.at[3])
    halves_in.wait_send()
    wait_bytes(plane_in.at[pl.ds(0, plane - 1)], sum_send.at[1])
    wait_bytes(line_in.at[pl.ds(0, line - 1)], sum_send.at[2])
    wait_bytes(pieces, sum_send.at[3])
    relay_done(0, *edge_refs(1)[1::2])
    relay_done(1, *rim_refs(1)[1::2])
    relay_done(2, *rim_refs(0)[1::2])
    for layer in range(2):
        sent(edge_copies(layer))
        sent(rim_copies(layer))
        for part in range(2):
            sent(row_copies(layer, part))
            sent(fold_copies(layer, part))
    wait_bytes(gathered.at[1 - core], sum_recv.at[4])
    wait_bytes(gathered.at[1 - core], sum_send.at[4])
    probe_out[...] = gathered[...].reshape(probe_out.shape)


def solution(mesh):
    rows, cols = mesh.shape["row"], mesh.shape["col"]

    def shards(transmission, probe, prop_phase, intensity, offsets, counts):
        slots = offsets.shape[0]
        f32 = jnp.float32
        plane = rows // (2 * Z_LOW) * Y_SIDE
        line = Z_LOW * (cols // Y_SIDE)
        depth = SIDE // plane
        hbm = pl.BlockSpec(memory_space=pltpu.HBM)
        smem = pl.BlockSpec(memory_space=pltpu.SMEM)
        vmem = pl.BlockSpec(memory_space=pltpu.VMEM)
        dma = pltpu.SemaphoreType.DMA
        return pl.pallas_call(
            functools.partial(kernel, rows, cols, slots * rows * cols),
            out_shape=(
                jax.ShapeDtypeStruct(transmission.shape, f32),
                jax.ShapeDtypeStruct(probe.shape, f32),
            ),
            in_specs=[smem, smem] + [hbm] * 4,
            out_specs=(vmem, vmem),
            scratch_shapes=[
                pltpu.VMEM((2, TILES, 3 * HALF, SIDE), f32),
                pltpu.VMEM((2, TILES, 3 * HALF, SIDE), f32),
                pltpu.VMEM((3, 2, HALF // Y_SIDE, SIDE), f32),
                pltpu.VMEM(probe.shape, f32),
                pltpu.VMEM(prop_phase.shape, f32),
                pltpu.VMEM(intensity.shape, intensity.dtype),
                pltpu.VMEM((4, 2 * SIDE, 2 * SIDE), jnp.bfloat16),
                pltpu.VMEM((2, 2, HALF, SIDE), f32),
                pltpu.VMEM((2, 2, HALF, SIDE), f32),
                pltpu.VMEM((2, 2, slots * SIDE, SIDE), f32),
                pltpu.VMEM((2, slots * SIDE, SIDE), f32),
                pltpu.VMEM((2, SIDE, SIDE), f32),
                pltpu.VMEM((2, 2, slots, 3, 4 * HALF, SIDE), f32),
                pltpu.VMEM((2, 2, TILES, 3 * HALF, SIDE), f32),
                pltpu.VMEM((2, 2, 2, TILES, HALF, SIDE), f32),
                pltpu.VMEM((2, 2, HALF, SIDE), f32),
                pltpu.VMEM((2, 2, HALF, SIDE), f32),
                pltpu.VMEM((2, SIDE, SIDE), f32),
                pltpu.VMEM((SIDE, SIDE), f32),
                pltpu.VMEM((plane, depth, SIDE), f32),
                pltpu.VMEM((plane, depth, SIDE), f32),
                pltpu.VMEM((line, depth, SIDE), f32),
                pltpu.VMEM((2, plane, depth, SIDE), f32),
                dma((7,)),
                dma((2, 2)),
                dma((2, 2)),
                dma((2, 2, 2)),
                dma((2, 2, 2)),
                dma((2, 2, 2)),
                dma((2, 2, 2)),
                dma((2, 2)),
                dma((2, 2)),
                dma((5,)),
                dma((5,)),
                pltpu.SemaphoreType.REGULAR((3,)),
                dma((3, 2)),
                dma((3, 2)),
            ],
            compiler_params=pltpu.CompilerParams(
                collective_id=0, has_side_effects=True, vmem_limit_bytes=60 * 1024 * 1024
            ),
        )(offsets.T, counts, transmission, probe, prop_phase, intensity)

    in_specs = (
        P(None, None, "row", "col"),
        P(),
        P(),
        P(("row", "col"), None, None),
        P(("row", "col"), None),
        P(("row", "col")),
    )
    out_specs = (P(None, None, "row", "col"), P())
    return jax.shard_map(shards, mesh=mesh, in_specs=in_specs, out_specs=out_specs, check_vma=False)
```

```python
import functools
import math

import jax
import jax.numpy as jnp
from jax import lax
from jax.experimental import pallas as pl
from jax.experimental.pallas import tpu as pltpu
from jax.sharding import PartitionSpec as P

MESH = pl.DeviceIdType.MESH
SIDE = 128
HALF = 64
TILES = 3
Z_LOW = 4
Y_SIDE = 4


def dft_tables():
    rows = lax.broadcasted_iota(jnp.int32, (SIDE, SIDE), 0)
    lanes = lax.broadcasted_iota(jnp.int32, (SIDE, SIDE), 1)
    angles = lax.rem(rows * lanes, SIDE).astype(jnp.float32) * (-2.0 * math.pi / SIDE)
    re, im = jnp.cos(angles) * (1.0 / math.sqrt(SIDE)), jnp.sin(angles) * (1.0 / math.sqrt(SIDE))
    block = lambda a, b, c, d: jnp.concatenate(
        [jnp.concatenate([a, b], axis=1), jnp.concatenate([c, d], axis=1)], axis=0
    )
    return block(re, im, -im, re), block(re, -im, im, re)


def halves(value):
    high = value.astype(jnp.bfloat16)
    return high, (value - high.astype(jnp.float32)).astype(jnp.bfloat16)


def product(left, right):
    dot = functools.partial(jnp.dot, preferred_element_type=jnp.float32)
    return dot(left[0], right[0]) + dot(left[1], right[0]) + dot(left[0], right[1])


def along_lanes(re, im, table):
    out = product(halves(jnp.concatenate([re, im], axis=1)), table)
    return out[:, :SIDE], out[:, SIDE:]


def along_rows(re, im, table):
    slots = re.shape[0] // SIDE
    beside = lambda part: jnp.concatenate([part[s * SIDE : (s + 1) * SIDE] for s in range(slots)], axis=1)
    out = product(table, halves(jnp.concatenate([beside(re), beside(im)], axis=0)))
    below = lambda part: jnp.concatenate([part[:, s * SIDE : (s + 1) * SIDE] for s in range(slots)], axis=0)
    return below(out[:SIDE]), below(out[SIDE:])


def times(a_re, a_im, b_re, b_im):
    return a_re * b_re - a_im * b_im, a_re * b_im + a_im * b_re


def times_conj(a_re, a_im, b_re, b_im):
    return a_re * b_re + a_im * b_im, a_im * b_re - a_re * b_im


def remote(src, dst, send, recv, device):
    return pltpu.make_async_remote_copy(
        src_ref=src, dst_ref=dst, send_sem=send, recv_sem=recv, device_id=device, device_id_type=MESH
    )


def kernel(
    rows, cols, total_slots,
    offsets, counts, trans, probe_in, phase_in, intensity_in,
    object_out, probe_out,
    ext_first, ext_second, relay_in, probe, phase, intensity, tables, edge_out, edge_in, patch, wave, prop, place, grid, fold_in, rim_out, rim_in,
    result, sum_out, plane_in, line_in, gathered,
    load_sem, store_sem, edge_send, edge_recv, row_send, row_recv, fold_send, fold_recv, rim_send, rim_recv, sum_send, sum_recv, line_sem, relay_send, relay_recv,
):
    ext = (ext_first, ext_second)
    slots = intensity.shape[0]
    row, col = lax.axis_index("row"), lax.axis_index("col")
    up, down = lax.rem(row + rows - 1, rows), lax.rem(row + 1, rows)
    left, right = lax.rem(col + cols - 1, cols), lax.rem(col + 1, cols)
    lane = lax.broadcasted_iota(jnp.int32, (HALF, SIDE), 1)
    low = lane < HALF
    own = slice(HALF, 2 * HALF)

    own_loads = [
        [
            pltpu.make_async_copy(
                trans.at[:, layer, :, pl.ds(tile * SIDE, SIDE)], ext[layer].at[:, tile, own, :], load_sem.at[layer * 2 + tile]
            )
            for tile in range(2)
        ]
        for layer in range(2)
    ]
    small_loads = [
        pltpu.make_async_copy(src, dst, load_sem.at[4 + i])
        for i, (src, dst) in enumerate(
            [(phase_in, phase), (probe_in, probe), (intensity_in, intensity)]
        )
    ]
    x_side, line = rows // (2 * Z_LOW), Z_LOW * (cols // Y_SIDE)
    plane = x_side * Y_SIDE
    x, z_low, core = lax.div(row, 2 * Z_LOW), lax.rem(lax.div(row, 2), Z_LOW), lax.rem(row, 2)
    y, z = lax.rem(col, Y_SIDE), lax.div(col, Y_SIDE) * Z_LOW + z_low
    spot_in_plane = x * Y_SIDE + y

    def plane_peer(k):
        to_x = lax.rem(x + lax.div(k, Y_SIDE), x_side)
        to_y = lax.rem(y + lax.rem(k, Y_SIDE), Y_SIDE)
        return to_x * Y_SIDE + to_y, {"row": (to_x * Z_LOW + z_low) * 2 + core, "col": col - y + to_y}

    def line_peer(k):
        to_z = lax.rem(z + k, line)
        return {"row": (x * Z_LOW + lax.rem(to_z, Z_LOW)) * 2 + core, "col": lax.div(to_z, Z_LOW) * Y_SIDE + y}

    def across(device):
        return {**device, "row": device["row"] + 1 - 2 * core}

    barrier = pltpu.get_barrier_semaphore()

    def greet(device):
        pl.semaphore_signal(barrier, inc=1, device_id=device, device_id_type=MESH)

    def greet_plane(k, _):
        greet(plane_peer(k)[1])
        greet(across(plane_peer(k)[1]))
        return 0

    for device in ({"row": up}, {"row": down}, {"col": left}, {"col": right}, line_peer(1), line_peer(line - 1)):
        greet(device)
    for layer in own_loads:
        for copy in layer:
            copy.start()
    for copy in small_loads:
        copy.start()
    lax.fori_loop(1, plane, greet_plane, 0)

    reaches = []
    while 2 ** len(reaches) < line // 2:
        reaches.append(2 ** len(reaches))

    def line_signal(turn):
        if turn < len(reaches):
            for k in (reaches[turn], line - reaches[turn]):
                pl.semaphore_signal(line_sem.at[turn], inc=1, device_id=line_peer(k), device_id_type=MESH)

    def line_wait(turn):
        if turn < len(reaches):
            pl.semaphore_wait(line_sem.at[turn], 2)

    def edge_copies(layer):
        return [
            remote(edge_out.at[layer, 0], edge_in.at[layer, 0], edge_send.at[layer, 0], edge_recv.at[layer, 0], {"col": right}),
            remote(edge_out.at[layer, 1], edge_in.at[layer, 1], edge_send.at[layer, 1], edge_recv.at[layer, 1], {"col": left}),
        ]

    def row_copies(layer, part):
        tiles = slice(0, 2) if part == 0 else slice(2, 3)
        src = ext[layer].at[:, tiles, own, :]
        return [
            remote(
                src, ext[layer].at[:, tiles, 0:HALF, :],
                row_send.at[layer, part, 0], row_recv.at[layer, part, 0], {"row": down},
            ),
            remote(
                src, ext[layer].at[:, tiles, 2 * HALF : 3 * HALF, :],
                row_send.at[layer, part, 1], row_recv.at[layer, part, 1], {"row": up},
            ),
        ]

    depth = HALF // Y_SIDE
    part_rows = lambda k: pl.ds(pl.multiple_of(k * depth, depth), depth)
    seams = ((Y_SIDE - 1, 1, lax.rem(col - y + Y_SIDE, cols)), (0, -1, lax.rem(col - y - 1 + cols, cols)))

    def start_spread(turn, copies, out, into, send, recv):
        for way, (seam, step, _) in enumerate(seams):

            @pl.when(y != seam)
            def _(way=way):
                copies[way].start()

            @pl.when(y == seam)
            def _(way=way, seam=seam, step=step):
                for k in range(1, Y_SIDE):
                    device = {"col": col - y + (seam + step * k) % Y_SIDE}
                    remote(
                        out.at[way, part_rows(k)], relay_in.at[turn, way], send.at[way], relay_recv.at[turn, way], device
                    ).start()
                beyond = {"col": right if way == 0 else left}
                remote(out.at[way, part_rows(0)], into.at[way, part_rows(0)], send.at[way], recv.at[way], beyond).start()

    def relayed(turn, way, into, recv):
        seam, _, beyond = seams[way]
        k = y + 1 if way == 0 else lax.rem(Y_SIDE - y, Y_SIDE)
        k = lax.rem(k, Y_SIDE)
        return remote(
            relay_in.at[turn, way], into.at[way, part_rows(k)], relay_send.at[turn, way], recv.at[way], {"col": beyond}
        )

    def relay(turn, into, recv):
        for way, (seam, _, _) in enumerate(seams):

            @pl.when(y != seam)
            def _(way=way):
                here = relay_in.at[turn, way]
                pltpu.make_async_copy(here, here, relay_recv.at[turn, way]).wait()
                relayed(turn, way, into, recv).start()

    def relay_done(turn, into, recv):
        for way, (seam, _, _) in enumerate(seams):

            @pl.when(y != seam)
            def _(way=way):
                relayed(turn, way, into, recv).wait_send()

    edge_refs = lambda layer: (edge_out.at[layer], edge_in.at[layer], edge_send.at[layer], edge_recv.at[layer])
    rim_refs = lambda layer: (rim_out.at[layer], rim_in.at[layer], rim_send.at[layer], rim_recv.at[layer])

    def start(copies):
        for copy in copies:
            copy.start()

    def landed(copies):
        for copy in copies:
            copy.wait_recv()

    def sent(copies):
        for copy in copies:
            copy.wait_send()

    for layer in range(2):
        for copy in own_loads[layer]:
            copy.wait()
        edge_out[layer, 0] = jnp.where(
            low, pltpu.roll(ext[layer][1, 1, own, :], HALF, 1), ext[layer][0, 1, own, :]
        )
        edge_out[layer, 1] = jnp.where(
            low, ext[layer][0, 0, own, :], pltpu.roll(ext[layer][1, 0, own, :], HALF, 1)
        )
    pl.semaphore_wait(barrier, 2 * (plane - 1) + 6)
    start(edge_copies(0))
    start_spread(0, edge_copies(1), *edge_refs(1))
    start(row_copies(0, 0))
    line_signal(0)

    for i, table in enumerate(dft_tables()):
        tables[2 * i], tables[2 * i + 1] = halves(table)
    for copy in small_loads:
        copy.wait()
    prop[0] = jnp.cos(phase[...])
    prop[1] = jnp.sin(phase[...])
    place[:, :, :, 0:2, 0:HALF, :] = jnp.zeros(place.shape[:3] + (2, HALF, SIDE), jnp.float32)
    place[:, :, :, 0:2, 3 * HALF :, :] = jnp.zeros(place.shape[:3] + (2, HALF, SIDE), jnp.float32)
    place[:, :, :, 2, :, :] = jnp.zeros(place.shape[:3] + (4 * HALF, SIDE), jnp.float32)
    relay(0, *edge_refs(1)[1::2])
    line_wait(0)
    line_signal(1)

    for layer in range(2):
        landed(edge_copies(layer))
        from_left = jnp.where(col > 0, edge_in[layer, 0], 0.0)
        from_right = jnp.where(col < cols - 1, edge_in[layer, 1], 0.0)
        ext[layer][0, 2, own, :] = jnp.where(low, from_right, from_left)
        ext[layer][1, 2, own, :] = pltpu.roll(jnp.where(low, from_left, from_right), HALF, 1)
        start(row_copies(layer, 1))
        if layer == 0:
            start(row_copies(1, 0))
    line_wait(1)
    line_signal(2)

    lanes = lax.broadcasted_iota(jnp.int32, (SIDE, SIDE), 1)

    def spot(slot):
        across = offsets[1, slot] + (TILES * SIDE - HALF)
        tile = lax.rem(lax.div(across, SIDE), TILES)
        return offsets[0, slot], tile, lax.rem(tile + 1, TILES), lax.rem(across, SIDE)

    spots = [spot(slot) for slot in range(slots)]

    def rows_arrived(layer):
        landed(row_copies(layer, 0))
        landed(row_copies(layer, 1))

        @pl.when(row == 0)
        def _():
            ext[layer][:, :, 0:HALF, :] = jnp.zeros((2, TILES, HALF, SIDE), jnp.float32)

        @pl.when(row == rows - 1)
        def _():
            ext[layer][:, :, 2 * HALF :, :] = jnp.zeros((2, TILES, HALF, SIDE), jnp.float32)

    def gather(layer):
        for slot, (top, tile, after, shift) in enumerate(spots):
            back = lax.rem(SIDE - shift, SIDE)
            for part in range(2):
                first = ext[layer][part, tile, pl.ds(top, SIDE), :]
                second = ext[layer][part, after, pl.ds(top, SIDE), :]
                patch[layer, part, slot * SIDE : (slot + 1) * SIDE, :] = pltpu.roll(
                    jnp.where(lanes < shift, second, first), back, 1
                )

    def scatter(layer, grad):
        for slot, (_, _, _, shift) in enumerate(spots):
            for part in range(2):
                moved = pltpu.roll(grad[part][slot * SIDE : (slot + 1) * SIDE], shift, 1)
                place[layer, part, slot, 0, HALF : 3 * HALF, :] = jnp.where(lanes < shift, 0.0, moved)
                place[layer, part, slot, 1, HALF : 3 * HALF, :] = jnp.where(lanes < shift, moved, 0.0)
        for tile in reversed(range(TILES)):
            for part in range(2):
                total = None
                for slot, (top, first, second, _) in enumerate(spots):
                    which = jnp.where(first == tile, 0, jnp.where(second == tile, 1, 2))
                    term = place[layer, part, slot, which, pl.ds(HALF - top, 3 * HALF), :]
                    total = term if total is None else total + term
                grid[layer, part, tile] = total
            if tile == 2:
                start(fold_copies(layer, 1))
        if layer == 1:
            start(fold_copies(layer, 0))

    def fold_copies(layer, part):
        tiles = slice(0, 2) if part == 0 else slice(2, 3)
        return [
            remote(
                grid.at[layer, :, tiles, 2 * HALF : 3 * HALF, :], fold_in.at[layer, 0, :, tiles],
                fold_send.at[layer, part, 0], fold_recv.at[layer, part, 0], {"row": down},
            ),
            remote(
                grid.at[layer, :, tiles, 0:HALF, :], fold_in.at[layer, 1, :, tiles],
                fold_send.at[layer, part, 1], fold_recv.at[layer, part, 1], {"row": up},
            ),
        ]

    def rim_copies(layer):
        return [
            remote(rim_out.at[layer, 0], rim_in.at[layer, 0], rim_send.at[layer, 0], rim_recv.at[layer, 0], {"col": right}),
            remote(rim_out.at[layer, 1], rim_in.at[layer, 1], rim_send.at[layer, 1], rim_recv.at[layer, 1], {"col": left}),
        ]

    repeat = lambda part: jnp.concatenate([part] * slots, axis=0)
    wide = (tables[0], tables[1])
    tall = (tables[2], tables[3])

    def transform(field):
        return along_rows(*along_lanes(*field, wide), tall)

    def inverse(field):
        return along_rows(*along_lanes(*field, tall), wide)

    shone = (repeat(probe[0]), repeat(probe[1]))
    moved = (repeat(prop[0]), repeat(prop[1]))

    rows_arrived(0)
    gather(0)
    field = times(*shone, patch[0, 0], patch[0, 1])
    field = inverse(times(*transform(field), *moved))
    wave[0] = field[0]
    wave[1] = field[1]
    rows_arrived(1)
    gather(1)
    far = transform(times(*field, patch[1, 0], patch[1, 1]))
    live = jnp.concatenate(
        [jnp.full((SIDE, SIDE), jnp.where(slot < counts[0], 2.0, 0.0), jnp.float32) for slot in range(slots)], axis=0
    )
    measured = jnp.concatenate([intensity[slot].astype(jnp.float32) for slot in range(slots)], axis=0)
    excess = (far[0] * far[0] + far[1] * far[1] - measured) * live
    back = inverse((far[0] * excess, far[1] * excess))
    scatter(1, times_conj(*back, wave[0], wave[1]))
    back = transform(times_conj(*back, patch[1, 0], patch[1, 1]))
    back = inverse(times_conj(*back, *moved))
    probe_grad = times_conj(*back, patch[0, 0], patch[0, 1])

    scale = 1.0 / math.sqrt(total_slots)
    for part in range(2):
        acc = probe_grad[part][:SIDE]
        for slot in range(1, slots):
            acc = acc + probe_grad[part][slot * SIDE : (slot + 1) * SIDE]
        sum_out[part] = (acc * scale).reshape(sum_out.shape[1:])

    def wait_bytes(ref, sem):
        pltpu.make_async_copy(ref, ref, sem).wait()

    hops = lambda k, count: min(k, count - k)
    line_order = sorted(range(1, line), key=lambda k: -hops(k, line))
    plane_order = sorted(range(1, plane), key=lambda k: -hops(k // Y_SIDE, x_side) - hops(k % Y_SIDE, Y_SIDE))

    def start_all(copy, order):
        for k in order:
            copy(k).start()

    def scatter_piece(k):
        index, device = plane_peer(k)
        return remote(sum_out.at[core, index], plane_in.at[from_here], sum_send.at[0], sum_recv.at[0], device)

    def scatter_across(k):
        index, device = plane_peer(k)
        return remote(sum_out.at[1 - core, index], plane_in.at[from_here], sum_send.at[0], sum_recv.at[0], across(device))

    def share_piece(k):
        return remote(line_in.at[z], line_in.at[z], sum_send.at[1], sum_recv.at[1], line_peer(k))

    def spread_piece(k):
        mine = gathered.at[core, spot_in_plane]
        return remote(mine, mine, sum_send.at[2], sum_recv.at[2], plane_peer(k)[1])

    def spread_across(k):
        mine = gathered.at[core, spot_in_plane]
        return remote(mine, mine, sum_send.at[3], sum_recv.at[3], across(plane_peer(k)[1]))

    def fold(layer, tile, part):
        above = jnp.where(row > 0, fold_in[layer, 0, part, tile], 0.0)
        below = jnp.where(row < rows - 1, fold_in[layer, 1, part, tile], 0.0)
        return grid[layer, part, tile, own, :] + above + below

    def store(layer):
        return pltpu.make_async_copy(result.at[layer], object_out.at[:, layer], store_sem.at[layer])

    def fold_rims(layer):
        landed(fold_copies(layer, 1))
        re, im = fold(layer, 2, 0), fold(layer, 2, 1)
        turned = pltpu.roll(im, HALF, 1)
        rim_out[layer, 0] = jnp.where(low, re, turned)
        rim_out[layer, 1] = jnp.where(low, turned, re)
        start_spread(2 - layer, rim_copies(layer), *rim_refs(layer))

    def fold_tiles(layer):
        landed(fold_copies(layer, 0))
        landed(rim_copies(layer))
        from_left = jnp.where(col > 0, rim_in[layer, 0], 0.0)
        from_right = jnp.where(col < cols - 1, rim_in[layer, 1], 0.0)
        for part in range(2):
            if part == 1:
                from_left, from_right = pltpu.roll(from_left, HALF, 1), pltpu.roll(from_right, HALF, 1)
            result[layer, part, :, 0:SIDE] = fold(layer, 0, part) + jnp.where(low, from_left, 0.0)
            result[layer, part, :, SIDE:] = fold(layer, 1, part) + jnp.where(low, 0.0, from_right)
        store(layer).start()

    from_here = core * plane + spot_in_plane
    start_all(scatter_piece, plane_order)
    start_all(scatter_across, plane_order + [0])
    scatter(0, times_conj(*back, *shone))
    fold_rims(1)
    relay(1, *rim_refs(1)[1::2])
    plane_in[from_here] = sum_out[core, spot_in_plane]
    wait_bytes(plane_in.at[pl.ds(0, 2 * plane - 1)], sum_recv.at[0])
    line_in[z] = jnp.sum(plane_in[...], axis=0)
    line_wait(2)
    start_all(share_piece, line_order)
    start(fold_copies(0, 0))
    fold_rims(0)
    fold_tiles(1)
    relay(2, *rim_refs(0)[1::2])
    wait_bytes(line_in.at[pl.ds(0, line - 1)], sum_recv.at[1])
    gathered[core, spot_in_plane] = jnp.sum(line_in[...], axis=0)
    start_all(spread_piece, plane_order)
    start_all(spread_across, plane_order + [0])
    fold_tiles(0)
    pieces = gathered.at[core, pl.ds(0, plane - 1)]
    wait_bytes(pieces, sum_recv.at[2])
    wait_bytes(plane_in.at[pl.ds(0, 2 * plane - 1)], sum_send.at[0])
    wait_bytes(line_in.at[pl.ds(0, line - 1)], sum_send.at[1])
    wait_bytes(pieces, sum_send.at[2])
    relay_done(0, *edge_refs(1)[1::2])
    relay_done(1, *rim_refs(1)[1::2])
    relay_done(2, *rim_refs(0)[1::2])
    for layer in range(2):
        sent(edge_copies(layer))
        sent(rim_copies(layer))
        for part in range(2):
            sent(row_copies(layer, part))
            sent(fold_copies(layer, part))
    wait_bytes(gathered.at[1 - core], sum_recv.at[3])
    wait_bytes(gathered.at[1 - core], sum_send.at[3])
    store_sum = pltpu.make_async_copy(gathered, probe_out, store_sem.at[2])
    store_sum.start()
    store(0).wait()
    store(1).wait()
    store_sum.wait()


def deliver(object_in, probe_in, object_out, probe_out, object_held, probe_held, sem):
    parts = [(object_in.at[i, j], object_held.at[i, j], object_out.at[i, j]) for i in range(2) for j in range(2)]
    parts += [(probe_in.at[i], probe_held.at[i], probe_out.at[i]) for i in range(2)]
    loads = [pltpu.make_async_copy(src, held, sem.at[0, i]) for i, (src, held, _) in enumerate(parts)]
    stores = [pltpu.make_async_copy(held, dst, sem.at[1, i]) for i, (_, held, dst) in enumerate(parts)]
    for load in loads:
        load.start()
    for load, store in zip(loads, stores):
        load.wait()
        store.start()
    for store in stores:
        store.wait()


def solution(mesh):
    rows, cols = mesh.shape["row"], mesh.shape["col"]

    def shards(transmission, probe, prop_phase, intensity, offsets, counts):
        slots = offsets.shape[0]
        f32 = jnp.float32
        plane = rows // (2 * Z_LOW) * Y_SIDE
        line = Z_LOW * (cols // Y_SIDE)
        depth = SIDE // plane
        hbm = pl.BlockSpec(memory_space=pltpu.HBM)
        smem = pl.BlockSpec(memory_space=pltpu.SMEM)
        dma = pltpu.SemaphoreType.DMA
        outs = pl.pallas_call(
            functools.partial(kernel, rows, cols, slots * rows * cols),
            out_shape=(
                jax.ShapeDtypeStruct(transmission.shape, f32),
                jax.ShapeDtypeStruct((2, plane, depth, SIDE), f32),
            ),
            in_specs=[smem, smem] + [hbm] * 4,
            out_specs=(hbm, hbm),
            scratch_shapes=[
                pltpu.VMEM((2, TILES, 3 * HALF, SIDE), f32),
                pltpu.VMEM((2, TILES, 3 * HALF, SIDE), f32),
                pltpu.VMEM((3, 2, HALF // Y_SIDE, SIDE), f32),
                pltpu.VMEM(probe.shape, f32),
                pltpu.VMEM(prop_phase.shape, f32),
                pltpu.VMEM(intensity.shape, intensity.dtype),
                pltpu.VMEM((4, 2 * SIDE, 2 * SIDE), jnp.bfloat16),
                pltpu.VMEM((2, 2, HALF, SIDE), f32),
                pltpu.VMEM((2, 2, HALF, SIDE), f32),
                pltpu.VMEM((2, 2, slots * SIDE, SIDE), f32),
                pltpu.VMEM((2, slots * SIDE, SIDE), f32),
                pltpu.VMEM((2, SIDE, SIDE), f32),
                pltpu.VMEM((2, 2, slots, 3, 4 * HALF, SIDE), f32),
                pltpu.VMEM((2, 2, TILES, 3 * HALF, SIDE), f32),
                pltpu.VMEM((2, 2, 2, TILES, HALF, SIDE), f32),
                pltpu.VMEM((2, 2, HALF, SIDE), f32),
                pltpu.VMEM((2, 2, HALF, SIDE), f32),
                pltpu.VMEM((2, 2, HALF, 2 * SIDE), f32),
                pltpu.VMEM((2, plane, depth, SIDE), f32),
                pltpu.VMEM((2 * plane, depth, SIDE), f32),
                pltpu.VMEM((line, depth, SIDE), f32),
                pltpu.VMEM((2, plane, depth, SIDE), f32),
                dma((7,)),
                dma((3,)),
                dma((2, 2)),
                dma((2, 2)),
                dma((2, 2, 2)),
                dma((2, 2, 2)),
                dma((2, 2, 2)),
                dma((2, 2, 2)),
                dma((2, 2)),
                dma((2, 2)),
                dma((4,)),
                dma((4,)),
                pltpu.SemaphoreType.REGULAR((3,)),
                dma((3, 2)),
                dma((3, 2)),
            ],
            compiler_params=pltpu.CompilerParams(
                collective_id=0, has_side_effects=True, vmem_limit_bytes=60 * 1024 * 1024
            ),
        )(offsets.T, counts, transmission, probe, prop_phase, intensity)
        return pl.pallas_call(
            deliver,
            out_shape=(
                jax.ShapeDtypeStruct(transmission.shape, f32),
                jax.ShapeDtypeStruct(probe.shape, f32),
            ),
            in_specs=[hbm, hbm],
            out_specs=(hbm, hbm),
            scratch_shapes=[pltpu.VMEM(transmission.shape, f32), pltpu.VMEM(probe.shape, f32), dma((2, 6))],
            compiler_params=pltpu.CompilerParams(vmem_limit_bytes=60 * 1024 * 1024),
        )(outs[0], outs[1].reshape(probe.shape))

    in_specs = (
        P(None, None, "row", "col"),
        P(),
        P(),
        P(("row", "col"), None, None),
        P(("row", "col"), None),
        P(("row", "col")),
    )
    out_specs = (P(None, None, "row", "col"), P())
    return jax.shard_map(shards, mesh=mesh, in_specs=in_specs, out_specs=out_specs, check_vma=False)
```

```python
import functools
import math

import jax
import jax.numpy as jnp
from jax import lax
from jax.experimental import pallas as pl
from jax.experimental.pallas import tpu as pltpu
from jax.sharding import PartitionSpec as P

MESH = pl.DeviceIdType.MESH
SIDE = 128
HALF = 64
TILES = 3
Z_LOW = 4
Y_SIDE = 4


def dft_tables():
    rows = lax.broadcasted_iota(jnp.int32, (SIDE, SIDE), 0)
    lanes = lax.broadcasted_iota(jnp.int32, (SIDE, SIDE), 1)
    angles = lax.rem(rows * lanes, SIDE).astype(jnp.float32) * (-2.0 * math.pi / SIDE)
    re, im = jnp.cos(angles) * (1.0 / math.sqrt(SIDE)), jnp.sin(angles) * (1.0 / math.sqrt(SIDE))
    block = lambda a, b, c, d: jnp.concatenate(
        [jnp.concatenate([a, b], axis=1), jnp.concatenate([c, d], axis=1)], axis=0
    )
    return block(re, im, -im, re), block(re, -im, im, re)


def halves(value):
    high = value.astype(jnp.bfloat16)
    return high, (value - high.astype(jnp.float32)).astype(jnp.bfloat16)


def product(left, right):
    dot = functools.partial(jnp.dot, preferred_element_type=jnp.float32)
    return dot(left[0], right[0]) + dot(left[1], right[0]) + dot(left[0], right[1])


def along_lanes(re, im, table):
    out = product(halves(jnp.concatenate([re, im], axis=1)), table)
    return out[:, :SIDE], out[:, SIDE:]


def along_rows(re, im, table):
    slots = re.shape[0] // SIDE
    beside = lambda part: jnp.concatenate([part[s * SIDE : (s + 1) * SIDE] for s in range(slots)], axis=1)
    out = product(table, halves(jnp.concatenate([beside(re), beside(im)], axis=0)))
    below = lambda part: jnp.concatenate([part[:, s * SIDE : (s + 1) * SIDE] for s in range(slots)], axis=0)
    return below(out[:SIDE]), below(out[SIDE:])


def times(a_re, a_im, b_re, b_im):
    return a_re * b_re - a_im * b_im, a_re * b_im + a_im * b_re


def times_conj(a_re, a_im, b_re, b_im):
    return a_re * b_re + a_im * b_im, a_im * b_re - a_re * b_im


def remote(src, dst, send, recv, device):
    return pltpu.make_async_remote_copy(
        src_ref=src, dst_ref=dst, send_sem=send, recv_sem=recv, device_id=device, device_id_type=MESH
    )


def kernel(
    rows, cols, total_slots,
    offsets, counts, trans, probe_in, phase_in, intensity_in,
    object_out, probe_out,
    ext_first, ext_second, relay_in, probe, phase, intensity, tables, edge_out, edge_in, patch, wave, prop, place, grid, fold_in, rim_out, rim_in,
    result, sum_out, plane_in, line_in, gathered,
    load_sem, store_sem, edge_send, edge_recv, row_send, row_recv, fold_send, fold_recv, rim_send, rim_recv, sum_send, sum_recv, line_sem, relay_send, relay_recv,
):
    ext = (ext_first, ext_second)
    slots = intensity.shape[0]
    row, col = lax.axis_index("row"), lax.axis_index("col")
    up, down = lax.rem(row + rows - 1, rows), lax.rem(row + 1, rows)
    left, right = lax.rem(col + cols - 1, cols), lax.rem(col + 1, cols)
    lane = lax.broadcasted_iota(jnp.int32, (HALF, SIDE), 1)
    low = lane < HALF
    own = slice(HALF, 2 * HALF)

    own_loads = [
        [
            pltpu.make_async_copy(
                trans.at[:, layer, :, pl.ds(tile * SIDE, SIDE)], ext[layer].at[:, tile, own, :], load_sem.at[layer * 2 + tile]
            )
            for tile in range(2)
        ]
        for layer in range(2)
    ]
    small_loads = [
        pltpu.make_async_copy(src, dst, load_sem.at[4 + i])
        for i, (src, dst) in enumerate(
            [(phase_in, phase), (probe_in, probe), (intensity_in, intensity)]
        )
    ]
    x_side, line = rows // (2 * Z_LOW), Z_LOW * (cols // Y_SIDE)
    plane = x_side * Y_SIDE
    x, z_low, core = lax.div(row, 2 * Z_LOW), lax.rem(lax.div(row, 2), Z_LOW), lax.rem(row, 2)
    y, z = lax.rem(col, Y_SIDE), lax.div(col, Y_SIDE) * Z_LOW + z_low
    spot_in_plane = x * Y_SIDE + y

    def plane_peer(k):
        to_x = lax.rem(x + lax.div(k, Y_SIDE), x_side)
        to_y = lax.rem(y + lax.rem(k, Y_SIDE), Y_SIDE)
        return to_x * Y_SIDE + to_y, {"row": (to_x * Z_LOW + z_low) * 2 + core, "col": col - y + to_y}

    def line_peer(k):
        to_z = lax.rem(z + k, line)
        return {"row": (x * Z_LOW + lax.rem(to_z, Z_LOW)) * 2 + core, "col": lax.div(to_z, Z_LOW) * Y_SIDE + y}

    def across(device):
        return {**device, "row": device["row"] + 1 - 2 * core}

    barrier = pltpu.get_barrier_semaphore()

    def greet(device):
        pl.semaphore_signal(barrier, inc=1, device_id=device, device_id_type=MESH)

    def greet_plane(k, _):
        greet(plane_peer(k)[1])
        greet(across(plane_peer(k)[1]))
        return 0

    for device in ({"row": up}, {"row": down}, {"col": left}, {"col": right}, line_peer(1), line_peer(line - 1)):
        greet(device)
    for layer in own_loads:
        for copy in layer:
            copy.start()
    for copy in small_loads:
        copy.start()
    lax.fori_loop(1, plane, greet_plane, 0)

    reaches = []
    while 2 ** len(reaches) < line // 2:
        reaches.append(2 ** len(reaches))

    def line_signal(turn):
        if turn < len(reaches):
            for k in (reaches[turn], line - reaches[turn]):
                pl.semaphore_signal(line_sem.at[turn], inc=1, device_id=line_peer(k), device_id_type=MESH)

    def line_wait(turn):
        if turn < len(reaches):
            pl.semaphore_wait(line_sem.at[turn], 2)

    def edge_copies(layer):
        return [
            remote(edge_out.at[layer, 0], edge_in.at[layer, 0], edge_send.at[layer, 0], edge_recv.at[layer, 0], {"col": right}),
            remote(edge_out.at[layer, 1], edge_in.at[layer, 1], edge_send.at[layer, 1], edge_recv.at[layer, 1], {"col": left}),
        ]

    def row_copies(layer, part):
        tiles = slice(0, 2) if part == 0 else slice(2, 3)
        src = ext[layer].at[:, tiles, own, :]
        return [
            remote(
                src, ext[layer].at[:, tiles, 0:HALF, :],
                row_send.at[layer, part, 0], row_recv.at[layer, part, 0], {"row": down},
            ),
            remote(
                src, ext[layer].at[:, tiles, 2 * HALF : 3 * HALF, :],
                row_send.at[layer, part, 1], row_recv.at[layer, part, 1], {"row": up},
            ),
        ]

    depth = HALF // Y_SIDE
    part_rows = lambda k: pl.ds(pl.multiple_of(k * depth, depth), depth)
    seams = ((Y_SIDE - 1, 1, lax.rem(col - y + Y_SIDE, cols)), (0, -1, lax.rem(col - y - 1 + cols, cols)))

    def start_spread(turn, copies, out, into, send, recv):
        for way, (seam, step, _) in enumerate(seams):

            @pl.when(y != seam)
            def _(way=way):
                copies[way].start()

            @pl.when(y == seam)
            def _(way=way, seam=seam, step=step):
                for k in range(1, Y_SIDE):
                    device = {"col": col - y + (seam + step * k) % Y_SIDE}
                    remote(
                        out.at[way, part_rows(k)], relay_in.at[turn, way], send.at[way], relay_recv.at[turn, way], device
                    ).start()
                beyond = {"col": right if way == 0 else left}
                remote(out.at[way, part_rows(0)], into.at[way, part_rows(0)], send.at[way], recv.at[way], beyond).start()

    def relayed(turn, way, into, recv):
        seam, _, beyond = seams[way]
        k = y + 1 if way == 0 else lax.rem(Y_SIDE - y, Y_SIDE)
        k = lax.rem(k, Y_SIDE)
        return remote(
            relay_in.at[turn, way], into.at[way, part_rows(k)], relay_send.at[turn, way], recv.at[way], {"col": beyond}
        )

    def relay(turn, into, recv):
        for way, (seam, _, _) in enumerate(seams):

            @pl.when(y != seam)
            def _(way=way):
                here = relay_in.at[turn, way]
                pltpu.make_async_copy(here, here, relay_recv.at[turn, way]).wait()
                relayed(turn, way, into, recv).start()

    def relay_done(turn, into, recv):
        for way, (seam, _, _) in enumerate(seams):

            @pl.when(y != seam)
            def _(way=way):
                relayed(turn, way, into, recv).wait_send()

    edge_refs = lambda layer: (edge_out.at[layer], edge_in.at[layer], edge_send.at[layer], edge_recv.at[layer])
    rim_refs = lambda layer: (rim_out.at[layer], rim_in.at[layer], rim_send.at[layer], rim_recv.at[layer])

    def start(copies):
        for copy in copies:
            copy.start()

    def landed(copies):
        for copy in copies:
            copy.wait_recv()

    def sent(copies):
        for copy in copies:
            copy.wait_send()

    def pack(layer):
        for copy in own_loads[layer]:
            copy.wait()
        edge_out[layer, 0] = jnp.where(
            low, pltpu.roll(ext[layer][1, 1, own, :], HALF, 1), ext[layer][0, 1, own, :]
        )
        edge_out[layer, 1] = jnp.where(
            low, ext[layer][0, 0, own, :], pltpu.roll(ext[layer][1, 0, own, :], HALF, 1)
        )

    pack(0)
    pl.semaphore_wait(barrier, 2 * (plane - 1) + 6)
    start(edge_copies(0))
    pack(1)
    start_spread(0, edge_copies(1), *edge_refs(1))
    start(row_copies(0, 0))
    line_signal(0)
    relay(0, *edge_refs(1)[1::2])

    for i, table in enumerate(dft_tables()):
        tables[2 * i], tables[2 * i + 1] = halves(table)
    for copy in small_loads:
        copy.wait()
    prop[0] = jnp.cos(phase[...])
    prop[1] = jnp.sin(phase[...])
    place[:, :, :, 0:2, 0:HALF, :] = jnp.zeros(place.shape[:3] + (2, HALF, SIDE), jnp.float32)
    place[:, :, :, 0:2, 3 * HALF :, :] = jnp.zeros(place.shape[:3] + (2, HALF, SIDE), jnp.float32)
    place[:, :, :, 2, :, :] = jnp.zeros(place.shape[:3] + (4 * HALF, SIDE), jnp.float32)
    line_wait(0)
    line_signal(1)

    for layer in range(2):
        landed(edge_copies(layer))
        from_left = jnp.where(col > 0, edge_in[layer, 0], 0.0)
        from_right = jnp.where(col < cols - 1, edge_in[layer, 1], 0.0)
        ext[layer][0, 2, own, :] = jnp.where(low, from_right, from_left)
        ext[layer][1, 2, own, :] = pltpu.roll(jnp.where(low, from_left, from_right), HALF, 1)
        start(row_copies(layer, 1))
        if layer == 0:
            start(row_copies(1, 0))
    line_wait(1)
    line_signal(2)

    lanes = lax.broadcasted_iota(jnp.int32, (SIDE, SIDE), 1)

    def spot(slot):
        across = offsets[1, slot] + (TILES * SIDE - HALF)
        tile = lax.rem(lax.div(across, SIDE), TILES)
        return offsets[0, slot], tile, lax.rem(tile + 1, TILES), lax.rem(across, SIDE)

    spots = [spot(slot) for slot in range(slots)]

    def rows_arrived(layer):
        landed(row_copies(layer, 0))
        landed(row_copies(layer, 1))

        @pl.when(row == 0)
        def _():
            ext[layer][:, :, 0:HALF, :] = jnp.zeros((2, TILES, HALF, SIDE), jnp.float32)

        @pl.when(row == rows - 1)
        def _():
            ext[layer][:, :, 2 * HALF :, :] = jnp.zeros((2, TILES, HALF, SIDE), jnp.float32)

    def gather(layer):
        for slot, (top, tile, after, shift) in enumerate(spots):
            back = lax.rem(SIDE - shift, SIDE)
            for part in range(2):
                first = ext[layer][part, tile, pl.ds(top, SIDE), :]
                second = ext[layer][part, after, pl.ds(top, SIDE), :]
                patch[layer, part, slot * SIDE : (slot + 1) * SIDE, :] = pltpu.roll(
                    jnp.where(lanes < shift, second, first), back, 1
                )

    def scatter(layer, grad):
        for slot, (_, _, _, shift) in enumerate(spots):
            for part in range(2):
                moved = pltpu.roll(grad[part][slot * SIDE : (slot + 1) * SIDE], shift, 1)
                place[layer, part, slot, 0, HALF : 3 * HALF, :] = jnp.where(lanes < shift, 0.0, moved)
                place[layer, part, slot, 1, HALF : 3 * HALF, :] = jnp.where(lanes < shift, moved, 0.0)
        for tile in reversed(range(TILES)):
            for part in range(2):
                total = None
                for slot, (top, first, second, _) in enumerate(spots):
                    which = jnp.where(first == tile, 0, jnp.where(second == tile, 1, 2))
                    term = place[layer, part, slot, which, pl.ds(HALF - top, 3 * HALF), :]
                    total = term if total is None else total + term
                grid[layer, part, tile] = total
            if tile == 2:
                start(fold_copies(layer, 1))
        if layer == 1:
            start(fold_copies(layer, 0))

    def fold_copies(layer, part):
        tiles = slice(0, 2) if part == 0 else slice(2, 3)
        return [
            remote(
                grid.at[layer, :, tiles, 2 * HALF : 3 * HALF, :], fold_in.at[layer, 0, :, tiles],
                fold_send.at[layer, part, 0], fold_recv.at[layer, part, 0], {"row": down},
            ),
            remote(
                grid.at[layer, :, tiles, 0:HALF, :], fold_in.at[layer, 1, :, tiles],
                fold_send.at[layer, part, 1], fold_recv.at[layer, part, 1], {"row": up},
            ),
        ]

    def rim_copies(layer):
        return [
            remote(rim_out.at[layer, 0], rim_in.at[layer, 0], rim_send.at[layer, 0], rim_recv.at[layer, 0], {"col": right}),
            remote(rim_out.at[layer, 1], rim_in.at[layer, 1], rim_send.at[layer, 1], rim_recv.at[layer, 1], {"col": left}),
        ]

    repeat = lambda part: jnp.concatenate([part] * slots, axis=0)
    wide = (tables[0], tables[1])
    tall = (tables[2], tables[3])

    def transform(field):
        return along_rows(*along_lanes(*field, wide), tall)

    def inverse(field):
        return along_rows(*along_lanes(*field, tall), wide)

    shone = (repeat(probe[0]), repeat(probe[1]))
    moved = (repeat(prop[0]), repeat(prop[1]))

    rows_arrived(0)
    gather(0)
    field = times(*shone, patch[0, 0], patch[0, 1])
    field = inverse(times(*transform(field), *moved))
    wave[0] = field[0]
    wave[1] = field[1]
    rows_arrived(1)
    gather(1)
    far = transform(times(*field, patch[1, 0], patch[1, 1]))
    live = jnp.concatenate(
        [jnp.full((SIDE, SIDE), jnp.where(slot < counts[0], 2.0, 0.0), jnp.float32) for slot in range(slots)], axis=0
    )
    measured = jnp.concatenate([intensity[slot].astype(jnp.float32) for slot in range(slots)], axis=0)
    excess = (far[0] * far[0] + far[1] * far[1] - measured) * live
    back = inverse((far[0] * excess, far[1] * excess))
    scatter(1, times_conj(*back, wave[0], wave[1]))
    back = transform(times_conj(*back, patch[1, 0], patch[1, 1]))
    back = inverse(times_conj(*back, *moved))
    probe_grad = times_conj(*back, patch[0, 0], patch[0, 1])

    scale = 1.0 / math.sqrt(total_slots)
    for part in range(2):
        acc = probe_grad[part][:SIDE]
        for slot in range(1, slots):
            acc = acc + probe_grad[part][slot * SIDE : (slot + 1) * SIDE]
        sum_out[part] = (acc * scale).reshape(sum_out.shape[1:])

    def wait_bytes(ref, sem):
        pltpu.make_async_copy(ref, ref, sem).wait()

    hops = lambda k, count: min(k, count - k)
    line_order = sorted(range(1, line), key=lambda k: -hops(k, line))
    plane_order = sorted(range(1, plane), key=lambda k: -hops(k // Y_SIDE, x_side) - hops(k % Y_SIDE, Y_SIDE))

    def start_all(copy, order):
        for k in order:
            copy(k).start()

    def scatter_piece(k):
        index, device = plane_peer(k)
        return remote(sum_out.at[core, index], plane_in.at[from_here], sum_send.at[0], sum_recv.at[0], device)

    def scatter_across(k):
        index, device = plane_peer(k)
        return remote(sum_out.at[1 - core, index], plane_in.at[from_here], sum_send.at[0], sum_recv.at[0], across(device))

    def share_piece(k):
        return remote(line_in.at[z], line_in.at[z], sum_send.at[1], sum_recv.at[1], line_peer(k))

    def spread_piece(k):
        mine = gathered.at[core, spot_in_plane]
        return remote(mine, mine, sum_send.at[2], sum_recv.at[2], plane_peer(k)[1])

    def spread_across(k):
        mine = gathered.at[core, spot_in_plane]
        return remote(mine, mine, sum_send.at[3], sum_recv.at[3], across(plane_peer(k)[1]))

    def fold(layer, tile, part):
        above = jnp.where(row > 0, fold_in[layer, 0, part, tile], 0.0)
        below = jnp.where(row < rows - 1, fold_in[layer, 1, part, tile], 0.0)
        return grid[layer, part, tile, own, :] + above + below

    def store(layer):
        return pltpu.make_async_copy(result.at[layer], object_out.at[:, layer], store_sem.at[layer])

    def fold_rims(layer):
        landed(fold_copies(layer, 1))
        re, im = fold(layer, 2, 0), fold(layer, 2, 1)
        turned = pltpu.roll(im, HALF, 1)
        rim_out[layer, 0] = jnp.where(low, re, turned)
        rim_out[layer, 1] = jnp.where(low, turned, re)
        start_spread(2 - layer, rim_copies(layer), *rim_refs(layer))

    def fold_tiles(layer):
        landed(fold_copies(layer, 0))
        landed(rim_copies(layer))
        from_left = jnp.where(col > 0, rim_in[layer, 0], 0.0)
        from_right = jnp.where(col < cols - 1, rim_in[layer, 1], 0.0)
        for part in range(2):
            if part == 1:
                from_left, from_right = pltpu.roll(from_left, HALF, 1), pltpu.roll(from_right, HALF, 1)
            result[layer, part, :, 0:SIDE] = fold(layer, 0, part) + jnp.where(low, from_left, 0.0)
            result[layer, part, :, SIDE:] = fold(layer, 1, part) + jnp.where(low, 0.0, from_right)
        store(layer).start()

    from_here = core * plane + spot_in_plane
    start_all(scatter_piece, plane_order)
    start_all(scatter_across, plane_order + [0])
    scatter(0, times_conj(*back, *shone))
    fold_rims(1)
    relay(1, *rim_refs(1)[1::2])
    plane_in[from_here] = sum_out[core, spot_in_plane]
    wait_bytes(plane_in.at[pl.ds(0, 2 * plane - 1)], sum_recv.at[0])
    line_in[z] = jnp.sum(plane_in[...], axis=0)
    line_wait(2)
    start_all(share_piece, line_order)
    start(fold_copies(0, 0))
    fold_rims(0)
    fold_tiles(1)
    relay(2, *rim_refs(0)[1::2])
    wait_bytes(line_in.at[pl.ds(0, line - 1)], sum_recv.at[1])
    gathered[core, spot_in_plane] = jnp.sum(line_in[...], axis=0)
    start_all(spread_piece, plane_order)
    start_all(spread_across, plane_order + [0])
    fold_tiles(0)
    pieces = gathered.at[core, pl.ds(0, plane - 1)]
    wait_bytes(pieces, sum_recv.at[2])
    wait_bytes(gathered.at[1 - core], sum_recv.at[3])
    store_sum = pltpu.make_async_copy(gathered, probe_out, store_sem.at[2])
    store_sum.start()
    wait_bytes(plane_in.at[pl.ds(0, 2 * plane - 1)], sum_send.at[0])
    wait_bytes(line_in.at[pl.ds(0, line - 1)], sum_send.at[1])
    wait_bytes(pieces, sum_send.at[2])
    wait_bytes(gathered.at[1 - core], sum_send.at[3])
    relay_done(2, *rim_refs(0)[1::2])
    relay_done(1, *rim_refs(1)[1::2])
    relay_done(0, *edge_refs(1)[1::2])
    for layer in range(2):
        sent(edge_copies(layer))
        sent(rim_copies(layer))
        for part in range(2):
            sent(row_copies(layer, part))
            sent(fold_copies(layer, part))
    store(0).wait()
    store(1).wait()
    store_sum.wait()


def deliver(object_in, probe_in, object_out, probe_out, object_held, probe_held, sem):
    parts = [(object_in.at[i, j], object_held.at[i, j], object_out.at[i, j]) for i in range(2) for j in range(2)]
    parts += [(probe_in.at[i], probe_held.at[i], probe_out.at[i]) for i in range(2)]
    loads = [pltpu.make_async_copy(src, held, sem.at[0, i]) for i, (src, held, _) in enumerate(parts)]
    stores = [pltpu.make_async_copy(held, dst, sem.at[1, i]) for i, (_, held, dst) in enumerate(parts)]
    for load in loads:
        load.start()
    for load, store in zip(loads, stores):
        load.wait()
        store.start()
    for store in stores:
        store.wait()


def solution(mesh):
    rows, cols = mesh.shape["row"], mesh.shape["col"]

    def shards(transmission, probe, prop_phase, intensity, offsets, counts):
        slots = offsets.shape[0]
        f32 = jnp.float32
        plane = rows // (2 * Z_LOW) * Y_SIDE
        line = Z_LOW * (cols // Y_SIDE)
        depth = SIDE // plane
        hbm = pl.BlockSpec(memory_space=pltpu.HBM)
        smem = pl.BlockSpec(memory_space=pltpu.SMEM)
        dma = pltpu.SemaphoreType.DMA
        outs = pl.pallas_call(
            functools.partial(kernel, rows, cols, slots * rows * cols),
            out_shape=(
                jax.ShapeDtypeStruct(transmission.shape, f32),
                jax.ShapeDtypeStruct((2, plane, depth, SIDE), f32),
            ),
            in_specs=[smem, smem] + [hbm] * 4,
            out_specs=(hbm, hbm),
            scratch_shapes=[
                pltpu.VMEM((2, TILES, 3 * HALF, SIDE), f32),
                pltpu.VMEM((2, TILES, 3 * HALF, SIDE), f32),
                pltpu.VMEM((3, 2, HALF // Y_SIDE, SIDE), f32),
                pltpu.VMEM(probe.shape, f32),
                pltpu.VMEM(prop_phase.shape, f32),
                pltpu.VMEM(intensity.shape, intensity.dtype),
                pltpu.VMEM((4, 2 * SIDE, 2 * SIDE), jnp.bfloat16),
                pltpu.VMEM((2, 2, HALF, SIDE), f32),
                pltpu.VMEM((2, 2, HALF, SIDE), f32),
                pltpu.VMEM((2, 2, slots * SIDE, SIDE), f32),
                pltpu.VMEM((2, slots * SIDE, SIDE), f32),
                pltpu.VMEM((2, SIDE, SIDE), f32),
                pltpu.VMEM((2, 2, slots, 3, 4 * HALF, SIDE), f32),
                pltpu.VMEM((2, 2, TILES, 3 * HALF, SIDE), f32),
                pltpu.VMEM((2, 2, 2, TILES, HALF, SIDE), f32),
                pltpu.VMEM((2, 2, HALF, SIDE), f32),
                pltpu.VMEM((2, 2, HALF, SIDE), f32),
                pltpu.VMEM((2, 2, HALF, 2 * SIDE), f32),
                pltpu.VMEM((2, plane, depth, SIDE), f32),
                pltpu.VMEM((2 * plane, depth, SIDE), f32),
                pltpu.VMEM((line, depth, SIDE), f32),
                pltpu.VMEM((2, plane, depth, SIDE), f32),
                dma((7,)),
                dma((3,)),
                dma((2, 2)),
                dma((2, 2)),
                dma((2, 2, 2)),
                dma((2, 2, 2)),
                dma((2, 2, 2)),
                dma((2, 2, 2)),
                dma((2, 2)),
                dma((2, 2)),
                dma((4,)),
                dma((4,)),
                pltpu.SemaphoreType.REGULAR((3,)),
                dma((3, 2)),
                dma((3, 2)),
            ],
            compiler_params=pltpu.CompilerParams(
                collective_id=0, has_side_effects=True, vmem_limit_bytes=60 * 1024 * 1024
            ),
        )(offsets.T, counts, transmission, probe, prop_phase, intensity)
        return pl.pallas_call(
            deliver,
            out_shape=(
                jax.ShapeDtypeStruct(transmission.shape, f32),
                jax.ShapeDtypeStruct(probe.shape, f32),
            ),
            in_specs=[hbm, hbm],
            out_specs=(hbm, hbm),
            scratch_shapes=[pltpu.VMEM(transmission.shape, f32), pltpu.VMEM(probe.shape, f32), dma((2, 6))],
            compiler_params=pltpu.CompilerParams(vmem_limit_bytes=60 * 1024 * 1024),
        )(outs[0], outs[1].reshape(probe.shape))

    in_specs = (
        P(None, None, "row", "col"),
        P(),
        P(),
        P(("row", "col"), None, None),
        P(("row", "col"), None),
        P(("row", "col")),
    )
    out_specs = (P(None, None, "row", "col"), P())
    return jax.shard_map(shards, mesh=mesh, in_specs=in_specs, out_specs=out_specs, check_vma=False)
```
